128 devices in a mesh: ctx: 8 (over y_lo, x), mdl: 16 (over z, y_hi, core).
Axes of the slice: x: 4, y: 4 (y_hi: 2, y_lo: 2; y = y_hi * 2 + y_lo), z: 4, core: 2. Of those that a mesh axis runs over, the one named last changes fastest.
Arguments:
- latents: bfloat16 [2048, 5120], P('ctx', 'mdl')
- mod_shift: float32 [5120], replicated, may hold values from -3 to 3
- mod_scale: float32 [5120], replicated, may hold values from -0.5 to 0.5
- gate: float32 [5120], replicated, may hold values from 0.3 to 3
- w_query: bfloat16 [5120, 4096], P(None, 'mdl'), may hold values from -0.15625 to 0.15625
- w_key: bfloat16 [5120, 4096], P(None, 'mdl'), may hold values from -0.078125 to 0.078125
- w_value: bfloat16 [5120, 4096], P(None, 'mdl'), may hold values from -0.078125 to 0.078125
- w_out: bfloat16 [4096, 5120], P('mdl'), may hold values from -0.75 to 0.75
- cache_keys: bfloat16 [4096, 4096], P('ctx', 'mdl'), may hold values from -610 to 610
- cache_values: bfloat16 [4096, 4096], P('ctx', 'mdl'), may hold values from -6 to 6
- final_scale: float32 [5120], replicated, may hold values from -0.5 to 0.5
- w_final: bfloat16 [5120, 64], replicated, may hold values from -0.078125 to 0.078125
- state: float32 [512, 256], P(('ctx', 'mdl')), may hold values from -6 to 6
- noise: float32 [512, 256], P(('ctx', 'mdl')), may hold values from -6 to 6
- owners: int32 [512, 1], P(('ctx', 'mdl')), may hold values from 0 to 15; in each aligned block of 4 rows (0 to 3, 4 to 7, ...) at most 2 rows name the same one
- w_up: bfloat16 [256, 1024], replicated, may hold values from -0.375 to 0.375
Outputs:
- hidden_out: bfloat16 [2048, 5120], P(('ctx', 'mdl'))
- next_state: float32 [512, 256], P(('ctx', 'mdl'))
- upsampled: bfloat16 [4096, 1024], P(('ctx', 'mdl'))
The draws below stay inside these ranges and needn't reach their ends.
Inputs may be any that keep to these rules, and one draw needn't show every extreme that they name: `owners`: among the 4 tiles of one device no owner is named more than 2 times, a bound that some block reaches.
All inputs are finite; a program needn't handle non-finite values.
Results may differ from the reference program's by a relative error of at most 0.039.
The reference program's roundings to bfloat16 on the way count: a program that leaves them out, or rounds other values in their place, can miss the bound.
Values may be sent and summed in bfloat16 or wider, within the bound.
No kernel may reach another device: no remote copies, remote signals or barrier semaphores. Data moves between devices by JAX's collectives and lax.ppermute only.
A program may use at most 128 MiB of HBM per device.

```python
import math
import jax
import jax.numpy as jnp
import numpy as np
from jax import lax

D = 5120
HD = 128
LAT = 64
CAP = 2
TILES_DEV = 4
HEADS = 32
TOKENS = 2048
PAST = 4096
TILES = 512
PANEL = 256
UP = 1024
N_CTX = 8
N_MDL = 16


def draw_latents(key, part):
    key = jax.random.fold_in(key, 11)
    key_cols, key_base = jax.random.split(key, 2)
    column_scale = jnp.exp(jax.random.uniform(key_cols, (1, D), jnp.float32, math.log(0.3), math.log(3.0)))
    values = jnp.clip(jax.random.normal(key_base, (TOKENS, D), jnp.float32), -6.0, 6.0) * column_scale
    return values.astype(jnp.bfloat16)


def draw_cache_keys(key, part):
    key = jax.random.fold_in(key, 23)
    base = jnp.clip(jax.random.normal(key, (PAST, HEADS * HD), jnp.float32), -5.0, 5.0)
    return base.astype(jnp.bfloat16)


def levels(own_key, shape, cuts, low, high):
    factor_of = 1.0
    for axis_at, shards_of in cuts:
        steps = jax.random.uniform(jax.random.fold_in(jax.random.fold_in(own_key, 6), axis_at), (shards_of,), jnp.float32, low / len(cuts), high / len(cuts))
        factor_of = factor_of * jnp.repeat(jnp.exp(steps), shape[axis_at] // shards_of).reshape((-1,) + (1,) * (len(shape) - 1 - axis_at))
    return factor_of


def deal_out(rng, own, number, rows, count, top, bound, slope):
    order = jax.random.permutation(rng, count)
    crowded, usual = shares(count, rows * top, bound, slope, True), shares(count, rows * top, bound, slope, False)
    places = jnp.arange(count)

    def named(lengths, offset_by):
        used = int((lengths > 0).sum())
        fixed = max(1, used // 4)
        shifted = fixed + (places - fixed + offset_by * (used - fixed)) % max(1, count - fixed)
        return jnp.zeros((count,), jnp.int32).at[order[jnp.where(places < fixed, places, shifted)]].set(jnp.asarray(lengths, jnp.int32))

    lengths = jnp.where(number % 4 == 0, named(crowded, number // 4), named(usual, number - number // 4 - 1))
    mixed = jax.random.permutation(jax.random.fold_in(own, 3), count)
    donor, taker = mixed[0:count // 2 * 2:2], mixed[1:count // 2 * 2:2]
    slack = jnp.minimum(lengths[donor] - 1, bound - lengths[taker]) // 2
    slack = jnp.where((donor == order[0]) | (taker == order[0]) | (lengths[taker] == 0), 0, jnp.maximum(slack, 0))
    shifted = jax.random.randint(jax.random.fold_in(own, 4), (count // 2,), 0, 1 << 20) % (slack + 1)
    lengths = lengths.at[donor].add(-shifted).at[taker].add(shifted)
    members = jnp.searchsorted(jnp.cumsum(lengths), jnp.arange(rows * top), side="right").astype(jnp.int32)
    table = members.reshape(top, rows).T
    table = table[jax.random.permutation(jax.random.fold_in(own, 1), rows)]
    offset_by = jax.random.randint(jax.random.fold_in(own, 2), (rows, 1), 0, top)
    return jnp.take_along_axis(table, (jnp.arange(top)[None, :] + offset_by) % top, axis=1)


def shares(count, total, most, skew, full):
    portions = [(1 << 20) // math.isqrt(rank ** skew) + 1 for rank in range(1, count + 1)]
    largest = most if full else min(most, max(-(-total // count), total * portions[0] // sum(portions)))
    least = 1 if total - largest >= count - 1 else 0
    holding, spare = [largest] + [least] * (count - 1), total - largest - least * (count - 1)
    while spare > 0:
        free = [i for i in range(1, count) if holding[i] < largest] or [i for i in range(1, count) if holding[i] < most]
        whole, remaining = sum([portions[i] for i in free]), spare
        for i in free:
            more = min(most - holding[i], max(1, remaining * portions[i] // whole), spare)
            holding[i] = holding[i] + more
            spare = spare - more
    return np.array(holding)


def scatter_about(stream_key, extent, spread, reach, shards=(), kind=jnp.bfloat16):
    entries = spread * jax.random.normal(stream_key, extent, jnp.float32)
    if shards:
        entries = entries * levels(stream_key, extent, shards, -0.22, 0.18)
    return jnp.clip(entries, -reach, reach).astype(kind)


def setup_inputs(seed: int = 0) -> dict:
    key_list = jax.random.split(jax.random.key(seed), 17)
    latents = draw_latents(jax.random.fold_in(key_list[16], 71), 0)
    mod_shift = scatter_about(key_list[1], (D,), 0.5, 3.0, (), jnp.float32)
    mod_scale = jnp.clip(jax.random.uniform(key_list[2], (D,), jnp.float32, -0.5, 0.5), -0.5, 0.5)
    gate = jnp.clip(jnp.exp(jax.random.uniform(key_list[3], (D,), jnp.float32, math.log(0.3), math.log(3.0))), 0.3, 3.0)
    w_query = scatter_about(key_list[4], (D, HEADS * HD), (D // 4) ** -0.5, 0.15625, ((1, 16),))
    w_key = scatter_about(key_list[5], (D, HEADS * HD), D ** -0.5, 0.078125, ((1, 16),))
    w_value = scatter_about(key_list[6], (D, HEADS * HD), D ** -0.5, 0.078125, ((1, 16),))
    w_out = scatter_about(key_list[7], (HEADS * HD, D), (HEADS * HD // 64) ** -0.5, 0.75, ((0, 16),))
    cache_keys = draw_cache_keys(jax.random.fold_in(key_list[16], 71), 0)
    cache_values = scatter_about(key_list[9], (PAST, HEADS * HD), 1.0, 6.0, ((0, 8), (1, 16)))
    final_scale = jnp.clip(jax.random.uniform(key_list[10], (D,), jnp.float32, -0.5, 0.5), -0.5, 0.5)
    w_final = scatter_about(key_list[11], (D, LAT), D ** -0.5, 0.078125)
    state = scatter_about(key_list[12], (TILES, PANEL), 1.0, 6.0, ((0, 128),), jnp.float32)
    noise = scatter_about(key_list[13], (TILES, PANEL), 1.0, 6.0, ((0, 128),), jnp.float32)
    owners_keys = jax.random.split(jax.random.fold_in(key_list[14], 1), TILES // TILES_DEV)
    owners_turns = jax.random.permutation(jax.random.fold_in(key_list[14], 3), TILES // TILES_DEV)
    owners = jax.vmap(lambda own, number: deal_out(jax.random.fold_in(key_list[14], 2), own, number, TILES_DEV, N_MDL, 1, CAP, 2))(owners_keys, owners_turns).reshape((TILES, 1))
    w_up = scatter_about(key_list[15], (PANEL, UP), PANEL ** -0.5, 0.375)
    return {"latents": latents, "mod_shift": mod_shift, "mod_scale": mod_scale, "gate": gate, "w_query": w_query, "w_key": w_key, "w_value": w_value, "w_out": w_out, "cache_keys": cache_keys, "cache_values": cache_values, "final_scale": final_scale, "w_final": w_final, "state": state, "noise": noise, "owners": owners, "w_up": w_up}


def reference(latents, mod_shift, mod_scale, gate, w_query, w_key, w_value, w_out, cache_keys, cache_values, final_scale, w_final, state, noise, owners, w_up):
    x_float = latents.astype(jnp.float32)
    row_mean = lax.optimization_barrier(jnp.mean(x_float, -1, keepdims=True))
    centred = x_float - row_mean
    row_var = lax.optimization_barrier(jnp.mean(centred * centred, -1, keepdims=True))
    normed_in = (centred * lax.rsqrt(row_var + 1e-06) * (1.0 + mod_scale) + mod_shift).astype(jnp.bfloat16)
    queries = jnp.dot(normed_in, w_query, preferred_element_type=jnp.float32).astype(jnp.bfloat16)
    keys_new = jnp.dot(normed_in, w_key, preferred_element_type=jnp.float32).astype(jnp.bfloat16)
    values_new = jnp.dot(normed_in, w_value, preferred_element_type=jnp.float32).astype(jnp.bfloat16)
    all_keys = jnp.concatenate([cache_keys, keys_new], 0)
    all_values = jnp.concatenate([cache_values, values_new], 0)
    heads = queries.shape[1] // HD
    query_heads = queries.reshape(TOKENS, heads, HD).transpose(1, 0, 2)
    key_heads = all_keys.reshape(PAST + TOKENS, heads, HD).transpose(1, 0, 2)
    value_heads = all_values.reshape(PAST + TOKENS, heads, HD).transpose(1, 0, 2)

    def one_head(operands):
        query_one, key_one, value_one = operands
        scores = jnp.dot(query_one, key_one.T, preferred_element_type=jnp.float32) / math.sqrt(HD)
        probs = jnp.exp(scores - lax.optimization_barrier(jnp.max(scores, -1, keepdims=True)))
        row_total = lax.optimization_barrier(jnp.sum(probs, -1, keepdims=True))
        summed = jnp.dot(probs.astype(jnp.bfloat16), value_one, preferred_element_type=jnp.float32)
        return (summed / row_total).astype(jnp.bfloat16)
    attended = lax.map(one_head, (query_heads, key_heads, value_heads))
    attended = attended.transpose(1, 0, 2).reshape(TOKENS, heads * HD)
    projected = jnp.dot(attended, w_out, preferred_element_type=jnp.float32)
    mixed = x_float + gate * projected
    hidden_out = mixed.astype(jnp.bfloat16)
    inverse = lax.rsqrt(lax.optimization_barrier(jnp.mean(mixed * mixed, -1, keepdims=True)) + 1e-06)
    normed_out = (mixed * inverse * (1.0 + final_scale)).astype(jnp.bfloat16)
    velocity = jnp.dot(normed_out, w_final, preferred_element_type=jnp.float32).reshape(TILES, PANEL)
    next_state = state + 0.2 * (velocity + 0.5 * (0.5 * velocity - state) / (1.0 - 0.5)) + math.sqrt(0.2) * noise
    panels = next_state.astype(jnp.bfloat16)
    devices = N_CTX * N_MDL
    grouped = owners[:, 0].reshape(devices, TILES_DEV)
    same = grouped[:, :, None] == grouped[:, None, :]
    earlier = jnp.arange(TILES_DEV)[None, :] < jnp.arange(TILES_DEV)[:, None]
    slots = lax.optimization_barrier(jnp.sum(jnp.logical_and(same, earlier[None, :, :]).astype(jnp.int32), -1)).astype(jnp.int32)
    device_ids = jnp.arange(devices, dtype=jnp.int32)[:, None]
    target = ((device_ids // N_MDL * N_MDL + grouped) * N_MDL + device_ids % N_MDL) * CAP + slots
    slot_rows = jnp.zeros((devices * N_MDL * CAP, PANEL), jnp.bfloat16).at[target.reshape(-1)].set(panels)
    upsampled = jax.nn.gelu(jnp.dot(slot_rows, w_up, preferred_element_type=jnp.float32)).astype(jnp.bfloat16)
    return (hidden_out, next_state, upsampled)
```

```python
import functools
import math

import jax
import jax.numpy as jnp
from jax import lax
from jax.experimental import pallas as pl
from jax.experimental.pallas import tpu as pltpu
from jax.sharding import PartitionSpec as P

HD = 128
CAP = 2
BF = jnp.bfloat16
F32 = jnp.float32
MIB = 1 << 20
VM = pl.BlockSpec(memory_space=pltpu.VMEM)
SM = pl.BlockSpec(memory_space=pltpu.SMEM)

CHIPS = [[2 * j + k for j in range(8)] for k in range(2)]
CORE_SWAP = [(m, m ^ 1) for m in range(16)]
Y_SWAP = [(c, c ^ 4) for c in range(8)]


def x_step(by):
    return [(c, (c // 4) * 4 + (c + by) % 4) for c in range(8)]


def core_swap(a):
    return lax.ppermute(a, "mdl", CORE_SWAP)


def chips_exchange(a):
    return lax.all_to_all(a, "mdl", 0, 0, axis_index_groups=CHIPS, tiled=True)


def call(body, outs, args, flops=0, nbytes=0, trans=0, smem=(), scratch=(), limit=32):
    return pl.pallas_call(
        body,
        out_shape=outs,
        in_specs=[SM if i in smem else VM for i in range(len(args))],
        out_specs=jax.tree.map(lambda o: VM, outs),
        scratch_shapes=list(scratch),
        compiler_params=pltpu.CompilerParams(vmem_limit_bytes=limit * MIB),
        cost_estimate=pl.CostEstimate(flops=flops, bytes_accessed=nbytes, transcendentals=trans),
    )(*args)


def shape(dims, dtype):
    return jax.ShapeDtypeStruct(dims, dtype)


def norm_body(x_ref, scale_ref, shift_ref, out_ref):
    blocks, rows, width = x_ref.shape
    total = jnp.zeros((rows, width), F32)
    for b in range(blocks):
        total = total + x_ref[b].astype(F32)
    mean = jnp.sum(total, -1, keepdims=True) / (blocks * width)
    square = jnp.zeros((rows, width), F32)
    for b in range(blocks):
        centred = x_ref[b].astype(F32) - mean
        square = square + centred * centred
    var = jnp.sum(square, -1, keepdims=True) / (blocks * width)
    inverse = lax.rsqrt(var + 1e-06)
    for b in range(blocks):
        centred = x_ref[b].astype(F32) - mean
        out_ref[b] = (
            centred * inverse * (1.0 + scale_ref[b : b + 1]) + shift_ref[b : b + 1]
        ).astype(BF)


def qkv_body(core_ref, own_ref, other_ref, wq_ref, wk_ref, wv_ref, q_ref, kv_ref, qa, kva):
    step = pl.program_id(0)
    k = core_ref[0]

    @pl.when(step == 0)
    def _():
        qa[...] = jnp.zeros_like(qa)
        kva[...] = jnp.zeros_like(kva)

    rows = own_ref.shape[1]
    own = own_ref[0]
    other = other_ref[0]
    first = jnp.where(k == 0, own, other)
    second = jnp.where(k == 0, other, own)
    x = jnp.concatenate([first, second], 0)
    qa[...] += jnp.dot(x, wq_ref[...], preferred_element_type=F32)
    kva[:, :256] += jnp.dot(x, wk_ref[...], preferred_element_type=F32)
    kva[:, 256:] += jnp.dot(x, wv_ref[...], preferred_element_type=F32)

    @pl.when(step == pl.num_programs(0) - 1)
    def _():
        q_ref[...] = qa[...].astype(BF)
        kv_ref[...] = kva[...].astype(BF)


def qkv_call(core, own, other, wq, wk, wv):
    blocks, rows, width = own.shape
    cols = wq.shape[1]
    w_spec = pl.BlockSpec((width, cols), lambda i: (i, 0))
    x_spec = pl.BlockSpec((1, rows, width), lambda i: (i, 0, 0))
    return pl.pallas_call(
        qkv_body,
        grid=(blocks,),
        out_shape=(shape((2 * rows, cols), BF), shape((2 * rows, 2 * cols), BF)),
        in_specs=[SM, x_spec, x_spec, w_spec, w_spec, w_spec],
        out_specs=(
            pl.BlockSpec((2 * rows, cols), lambda i: (0, 0)),
            pl.BlockSpec((2 * rows, 2 * cols), lambda i: (0, 0)),
        ),
        scratch_shapes=[pltpu.VMEM((2 * rows, cols), F32), pltpu.VMEM((2 * rows, 2 * cols), F32)],
        compiler_params=pltpu.CompilerParams(vmem_limit_bytes=24 * MIB),
        cost_estimate=pl.CostEstimate(
            flops=2 * 256 * 5120 * 768, bytes_accessed=10 * MIB, transcendentals=0
        ),
    )(core, own, other, wq, wk, wv)


C2 = math.log2(math.e) / math.sqrt(HD)


def attend(q_ref, kv_refs, start, h):
    q = q_ref[:, h * HD : (h + 1) * HD]
    peak, total, summed = start
    for kv in kv_refs:
        keys = kv[:, h * HD : (h + 1) * HD]
        values = kv[:, 256 + h * HD : 256 + (h + 1) * HD]
        s = lax.dot_general(q, keys, (((1,), (1,)), ((), ())), preferred_element_type=F32)
        here = jnp.max(s, -1, keepdims=True)
        new = here if peak is None else jnp.maximum(peak, here)
        p = jnp.exp2((s - new) * C2)
        t = jnp.sum(p, -1, keepdims=True)
        o = jnp.dot(p.astype(BF), values, preferred_element_type=F32)
        if peak is None:
            total, summed = t, o
        else:
            f = jnp.exp2((peak - new) * C2)
            total, summed = total * f + t, summed * f + o
        peak = new
    return peak, total, summed


def past_body(q_ref, a_ref, b_ref, c_ref, d_ref, o_ref, peak_ref, total_ref):
    for h in range(2):
        peak, total, summed = attend(
            q_ref, (a_ref, b_ref, c_ref, d_ref), (None, None, None), h
        )
        o_ref[:, h * HD : (h + 1) * HD] = summed
        peak_ref[h] = jnp.broadcast_to(peak, peak_ref.shape[1:])
        total_ref[h] = jnp.broadcast_to(total, total_ref.shape[1:])


def finish(q_ref, refs, o_ref, peak_ref, total_ref, h):
    start = (peak_ref[h][:, :1], total_ref[h][:, :1], o_ref[:, h * HD : (h + 1) * HD])
    peak, total, summed = attend(q_ref, refs, start, h)
    return summed / total, peak / math.sqrt(HD) + jnp.log(total)


def sent_body(q_ref, a_ref, b_ref, c_ref, d_ref, o_ref, peak_ref, total_ref, out_ref):
    rows = q_ref.shape[0]
    at = lax.broadcasted_iota(jnp.int32, (16, rows), 0)
    tail = jnp.zeros((16, rows), F32)
    for h in range(2):
        o, lse = finish(q_ref, (a_ref, b_ref, c_ref, d_ref), o_ref, peak_ref, total_ref, h)
        out_ref[:rows, h * HD : (h + 1) * HD] = o.astype(BF)
        rest = jnp.transpose(jnp.broadcast_to(lse, (rows, HD)))[:16]
        for i in range(3):
            piece = rest.astype(BF).astype(F32)
            tail = jnp.where(at == 3 * h + i, piece, tail)
            rest = rest - piece
    out_ref[rows:, :] = tail.astype(BF)


def kept_body(q_ref, a_ref, b_ref, c_ref, d_ref, o_ref, peak_ref, total_ref, out_ref, lse_ref):
    for h in range(2):
        o, lse = finish(q_ref, (a_ref, b_ref, c_ref, d_ref), o_ref, peak_ref, total_ref, h)
        out_ref[:, h * HD : (h + 1) * HD] = o
        lse_ref[h] = jnp.broadcast_to(lse, lse_ref.shape[1:])


def merge_body(own_ref, lse_ref, got_ref, out_ref):
    rows = own_ref.shape[0]
    tail = got_ref[rows:, :].astype(F32)
    for h in range(2):
        row = tail[3 * h : 3 * h + 1] + tail[3 * h + 1 : 3 * h + 2] + tail[3 * h + 2 : 3 * h + 3]
        theirs = jnp.transpose(jnp.broadcast_to(row, (HD, rows)))
        ours = lse_ref[h]
        top = jnp.maximum(ours, theirs)
        a, b = jnp.exp(ours - top), jnp.exp(theirs - top)
        cols = slice(h * HD, (h + 1) * HD)
        merged = (a * own_ref[:, cols] + b * got_ref[:rows, cols].astype(F32)) / (a + b)
        out_ref[:, cols] = merged.astype(BF)


def out_body(core_ref, own_ref, other_ref, wa_ref, wb_ref, out_ref):
    chips = out_ref.shape[0]
    width = out_ref.shape[2]
    for at in range(0, width, 512):
        cols = slice(at, at + 512)
        r = jnp.dot(own_ref[...], wa_ref[:, cols], preferred_element_type=F32) + jnp.dot(
            other_ref[...], wb_ref[:, cols], preferred_element_type=F32
        )
        r = r.astype(BF)
        for j in range(chips):
            out_ref[j, 0:16, cols] = r[16 * j : 16 * j + 16]
            out_ref[j, 16:32, cols] = r[128 + 16 * j : 128 + 16 * j + 16]


def sum_body(core_ref, got_ref, keep_ref, give_ref):
    k = core_ref[0]
    total = got_ref[0].astype(F32)
    for j in range(1, got_ref.shape[0]):
        total = total + got_ref[j].astype(F32)
    keep_ref[...] = jnp.where(k == 0, total[:16], total[16:])
    give_ref[...] = jnp.where(k == 0, total[16:], total[:16])


def tail_body(
    core_ref, own_ref, other_ref, x_ref, gate_ref, scale_ref, wf_ref, state_ref, noise_ref,
    owner_ref, hidden_ref, next_ref, slot_ref, vel,
):
    k = core_ref[0]
    own, other = own_ref[...], other_ref[...]
    left = jnp.where(k == 0, own, other)
    right = jnp.where(k == 0, other, own)
    blocks, rows, width = x_ref.shape
    half = blocks // 2
    mixed = []
    square = jnp.zeros((rows, width), F32)
    for b in range(blocks):
        at = (b % half) * width
        part = (left if b < half else right)[:, at : at + width]
        mix = x_ref[b].astype(F32) + gate_ref[b : b + 1] * part
        hidden_ref[:, b * width : (b + 1) * width] = mix.astype(BF)
        square = square + mix * mix
        mixed.append(mix)
    inverse = lax.rsqrt(jnp.sum(square, -1, keepdims=True) / (blocks * width) + 1e-06)
    acc = jnp.zeros(vel.shape, F32)
    for b in range(blocks):
        normed = (mixed[b] * inverse * (1.0 + scale_ref[b : b + 1])).astype(BF)
        acc = acc + jnp.dot(normed, wf_ref[b * width : (b + 1) * width], preferred_element_type=F32)
    vel[...] = acc
    tiles = state_ref.shape[0]
    lat = acc.shape[1]
    velocity = jnp.concatenate(
        [vel[pl.ds(j, tiles, stride=rows // tiles), :] for j in range(rows // tiles)], -1
    )
    state = state_ref[...]
    new = (
        state
        + 0.2 * (velocity + 0.5 * (0.5 * velocity - state) / (1.0 - 0.5))
        + math.sqrt(0.2) * noise_ref[...]
    )
    next_ref[...] = new
    panels = new.astype(BF).astype(F32)
    at = lax.broadcasted_iota(jnp.int32, slot_ref.shape, 0)
    slots = jnp.zeros(slot_ref.shape, F32)
    for t in range(tiles):
        owner = owner_ref[t]
        before = jnp.int32(0)
        for e in range(t):
            before = before + jnp.where(owner_ref[e] == owner, 1, 0)
        slots = jnp.where(at == owner * CAP + before, panels[t : t + 1], slots)
    slot_ref[...] = slots.astype(BF)


def up_body(x_ref, w_ref, out_ref):
    y = jnp.dot(x_ref[...], w_ref[...], preferred_element_type=F32)
    out_ref[...] = jax.nn.gelu(y).astype(BF)


def shards(
    latents, mod_shift, mod_scale, gate, w_query, w_key, w_value, w_out, cache_keys,
    cache_values, final_scale, w_final, state, noise, owners, w_up,
):
    count, part = latents.shape
    mdl = lax.axis_index("mdl")
    core = mdl % 2
    chip = mdl // 2
    core_1 = jnp.reshape(core, (1,)).astype(jnp.int32)
    chips = 8
    block = count // 16
    rows = count // 2

    split = latents.reshape(chips, 2, block, part)
    keep = lax.dynamic_index_in_dim(split, core, 1, keepdims=False).reshape(rows, part)
    give = lax.dynamic_index_in_dim(split, 1 - core, 1, keepdims=False).reshape(rows, part)
    got = core_swap(give)
    is_first = core == 0
    wide = jnp.concatenate(
        [jnp.where(is_first, keep, got), jnp.where(is_first, got, keep)], 1
    )
    x = chips_exchange(jnp.broadcast_to(wide[None], (chips, rows, 2 * part)))

    cached = jnp.concatenate([cache_keys, cache_values], 1)
    past = [cached] + [lax.ppermute(cached, "ctx", x_step(by)) for by in (1, 3, 2)]

    half = w_out.shape[1] // 2
    w_mine = lax.dynamic_slice_in_dim(w_out, core * half, half, 1)
    w_theirs = core_swap(lax.dynamic_slice_in_dim(w_out, (1 - core) * half, half, 1))

    normed = call(
        norm_body,
        shape(x.shape, BF),
        (x, mod_scale.reshape(chips, 2 * part), mod_shift.reshape(chips, 2 * part)),
        flops=10 * x.size,
        nbytes=4 * x.size,
    )
    query, kv = qkv_call(core_1, normed, core_swap(normed), w_query, w_key, w_value)
    fresh = [kv] + [lax.ppermute(kv, "ctx", x_step(by)) for by in (1, 3, 2)]
    query_in = lax.ppermute(query, "ctx", Y_SWAP)

    cols = query.shape[1]

    def past_call(q):
        return call(
            past_body,
            (
                shape((count, cols), F32),
                shape((2, count, HD), F32),
                shape((2, count, HD), F32),
            ),
            (q, *past),
            flops=4 * count * 2048 * 256,
            nbytes=4 * MIB,
            trans=count * 4096,
        )

    stats_own = past_call(query)
    stats_in = past_call(query_in)
    sent = call(
        sent_body,
        shape((count + 16, cols), BF),
        (query_in, *fresh, *stats_in),
        flops=4 * count * 1024 * 256,
        nbytes=2 * MIB,
        trans=count * 2048,
    )
    back = lax.ppermute(sent, "ctx", Y_SWAP)
    kept = call(
        kept_body,
        (shape((count, cols), F32), shape((2, count, HD), F32)),
        (query, *fresh, *stats_own),
        flops=4 * count * 1024 * 256,
        nbytes=2 * MIB,
        trans=count * 2048,
    )
    attended = call(merge_body, shape((count, cols), BF), (*kept, back), nbytes=MIB)

    projected = call(
        out_body,
        shape((chips, 2 * block, half), BF),
        (core_1, attended, core_swap(attended), w_mine, w_theirs),
        smem=(0,),
        flops=2 * count * 512 * half,
        nbytes=4 * MIB,
    )
    arrived = chips_exchange(projected)
    ours, theirs = call(
        sum_body,
        (shape((block, half), F32), shape((block, half), F32)),
        (core_1, arrived),
        smem=(0,),
        nbytes=2 * MIB,
    )
    own_x = lax.dynamic_slice_in_dim(x, chip * block, block, 1)
    hidden_out, next_state, slot_rows = call(
        tail_body,
        (
            shape((block, w_out.shape[1]), BF),
            shape(state.shape, F32),
            shape((16 * CAP, state.shape[1]), BF),
        ),
        (
            core_1, ours, core_swap(theirs), own_x, gate.reshape(chips, 2 * part),
            final_scale.reshape(chips, 2 * part), w_final, state, noise, owners[:, 0],
        ),
        smem=(0, 9),
        nbytes=2 * MIB,
        scratch=[pltpu.VMEM((block, w_final.shape[1]), F32)],
    )
    routed = lax.all_to_all(
        slot_rows.reshape(16, CAP, state.shape[1]), "mdl", split_axis=0, concat_axis=0, tiled=True
    ).reshape(16 * CAP, state.shape[1])
    upsampled = call(
        up_body, shape((16 * CAP, w_up.shape[1]), BF), (routed, w_up), nbytes=MIB
    )
    return (hidden_out, next_state, upsampled)


def solution(mesh):
    return jax.shard_map(
        shards,
        mesh=mesh,
        in_specs=(
            P("ctx", "mdl"),
            P(),
            P(),
            P(),
            P(None, "mdl"),
            P(None, "mdl"),
            P(None, "mdl"),
            P("mdl", None),
            P("ctx", "mdl"),
            P("ctx", "mdl"),
            P(),
            P(),
            P(("ctx", "mdl"), None),
            P(("ctx", "mdl"), None),
            P(("ctx", "mdl"), None),
            P(),
        ),
        out_specs=(P(("ctx", "mdl"), None), P(("ctx", "mdl"), None), P(("ctx", "mdl"), None)),
        check_vma=False,
    )
```

```python
import functools
import math

import jax
import jax.numpy as jnp
from jax import lax
from jax.experimental import pallas as pl
from jax.experimental.pallas import tpu as pltpu
from jax.sharding import PartitionSpec as P

HD = 128
CAP = 2
BF = jnp.bfloat16
F32 = jnp.float32
MIB = 1 << 20
VM = pl.BlockSpec(memory_space=pltpu.VMEM)
SM = pl.BlockSpec(memory_space=pltpu.SMEM)
HB = pl.BlockSpec(memory_space=pltpu.HBM)

CORE_SWAP = [(m, m ^ 1) for m in range(16)]
Y_SWAP = [(c, c ^ 4) for c in range(8)]
PAIR_SWAP = [(m, m ^ 2) for m in range(16)]
STEPS = (1, 3, 2)


def x_step(by):
    return [(c, (c // 4) * 4 + (c + by) % 4) for c in range(8)]


def core_swap(a):
    return lax.ppermute(a, "mdl", CORE_SWAP)


def z_send(a, by):
    return lax.ppermute(a, "mdl", [(m, (m + 4 * by) % 16) for m in range(16)])


def slot_chips(mdl, back):
    z, h = mdl >> 2, (mdl >> 1) & 1
    around = [(z + (-by if back else by)) & 3 for by in STEPS]
    return [z * 2 + h, z * 2 + 1 - h] + [a * 2 + h for a in around] + [a * 2 + 1 - h for a in around]


def call(
    body, outs, args, flops=0, nbytes=0, trans=0, smem=(), hbm=(), scratch=(), limit=24, after=()
):
    count = len(args)
    place = [SM if i in smem else HB if i in hbm else VM for i in range(count)]

    def run(*refs):
        body(*refs[:count], *refs[count + len(after) :])

    return pl.pallas_call(
        run,
        out_shape=outs,
        in_specs=place
        + [pl.BlockSpec(memory_space=pl.ANY)] * len(after),
        out_specs=jax.tree.map(lambda o: VM, outs),
        scratch_shapes=list(scratch),
        compiler_params=pltpu.CompilerParams(vmem_limit_bytes=limit * MIB),
        cost_estimate=pl.CostEstimate(flops=flops, bytes_accessed=nbytes, transcendentals=trans),
    )(*args, *after)


def shape(dims, dtype):
    return jax.ShapeDtypeStruct(dims, dtype)


def turn_body(core_ref, x_ref, keep_ref, give_ref):
    k = core_ref[0]
    block = 16
    x = jnp.transpose(x_ref[...])
    for j in range(x.shape[0] // (2 * block)):
        first = x[2 * j * block : (2 * j + 1) * block]
        second = x[(2 * j + 1) * block : (2 * j + 2) * block]
        keep_ref[j * block : (j + 1) * block] = jnp.where(k == 0, first, second)
        give_ref[j * block : (j + 1) * block] = jnp.where(k == 0, second, first)


def join_body(a_ref, b_ref, *out_refs):
    width = a_ref.shape[1]
    for i, out_ref in enumerate(out_refs):
        some = out_ref.shape[0]
        out_ref[:, :width] = a_ref[i * some : (i + 1) * some]
        out_ref[:, width:] = b_ref[i * some : (i + 1) * some]


def load_body(*refs):
    *refs, sems = refs
    half = len(refs) // 2
    pieces = sems.shape[1]
    copies = []
    for i, (src, dst) in enumerate(zip(refs[:half], refs[half:])):
        some = src.shape[0] // pieces
        for j in range(pieces):
            rows = pl.ds(j * some, some)
            copies.append(pltpu.make_async_copy(src.at[rows], dst.at[rows], sems.at[i, j]))
    for copy in copies:
        copy.start()
    for copy in copies:
        copy.wait()


def halves_body(core_ref, w_ref, mine_ref, theirs_ref):
    k = core_ref[0]
    width = mine_ref.shape[1]
    mine_ref[...] = w_ref[:, pl.ds(pl.multiple_of(k * width, width), width)]
    theirs_ref[...] = w_ref[:, pl.ds(pl.multiple_of((1 - k) * width, width), width)]


def norm_body(mdl_ref, *refs):
    *x_refs, scale_ref, shift_ref, out_ref, own_ref = refs
    blocks = len(x_refs)
    rows, width = x_refs[0].shape
    total = sum(x_ref[...].astype(F32) for x_ref in x_refs)
    mean = jnp.sum(total, -1, keepdims=True) / (blocks * width)
    square = jnp.zeros((rows, width), F32)
    for x_ref in x_refs:
        centred = x_ref[...].astype(F32) - mean
        square = square + centred * centred
    var = jnp.sum(square, -1, keepdims=True) / (blocks * width)
    inverse = lax.rsqrt(var + 1e-06)
    chips = slot_chips(mdl_ref[0], True)
    block = own_ref.shape[1]
    here = pl.ds(pl.multiple_of(chips[0] * block, block), block)
    for chip, x_ref in zip(chips, x_refs):
        own_ref[chip] = x_ref[here, :]
        centred = x_ref[...].astype(F32) - mean
        scale, shift = scale_ref[pl.ds(chip, 1)], shift_ref[pl.ds(chip, 1)]
        cols = pl.ds(pl.multiple_of(chip * width, width), width)
        out_ref[:, cols] = (centred * inverse * (1.0 + scale) + shift).astype(BF)


def kv_body(core_ref, own_ref, other_ref, wk_ref, wv_ref, kv_ref, x):
    k = core_ref[0]
    rows = own_ref.shape[0]
    x[pl.ds(pl.multiple_of(k * rows, rows), rows), :] = own_ref[...]
    x[pl.ds(pl.multiple_of((1 - k) * rows, rows), rows), :] = other_ref[...]
    kv_ref[:, :256] = jnp.dot(x[...], wk_ref[...], preferred_element_type=F32).astype(BF)
    kv_ref[:, 256:] = jnp.dot(x[...], wv_ref[...], preferred_element_type=F32).astype(BF)


def query_body(x_ref, wq_ref, q_ref):
    q_ref[...] = jnp.dot(x_ref[...], wq_ref[...], preferred_element_type=F32).astype(BF)


C2 = math.log2(math.e) / math.sqrt(HD)


def fold(op, parts):
    return functools.reduce(
        op, [p[:, at : at + HD] for p in parts for at in range(0, p.shape[1], HD)]
    )


def attend(q_ref, kv_refs, start, h):
    q = q_ref[:, h * HD : (h + 1) * HD]
    scores = [
        lax.dot_general(
            q, kv[:, h * HD : (h + 1) * HD], (((1,), (1,)), ((), ())), preferred_element_type=F32
        )
        for kv in kv_refs
    ]
    peak = jnp.max(fold(jnp.maximum, scores), -1, keepdims=True)
    if start is not None:
        peak = jnp.maximum(peak, start[0])
    probs = [jnp.exp2((s - peak) * C2) for s in scores]
    total = jnp.sum(fold(jnp.add, probs), -1, keepdims=True)
    summed = sum(
        jnp.dot(
            p.astype(BF), kv[:, 256 + h * HD : 256 + (h + 1) * HD], preferred_element_type=F32
        )
        for p, kv in zip(probs, kv_refs)
    )
    if start is not None:
        factor = jnp.exp2((start[0] - peak) * C2)
        total, summed = start[1] * factor + total, start[2] * factor + summed
    return peak, total, summed


def past_body(q_ref, *refs):
    *kv_refs, o_ref, peak_ref, total_ref = refs
    for h in range(2):
        peak, total, summed = attend(q_ref, kv_refs, None, h)
        o_ref[:, h * HD : (h + 1) * HD] = summed
        peak_ref[h] = jnp.broadcast_to(peak, peak_ref.shape[1:])
        total_ref[h] = jnp.broadcast_to(total, total_ref.shape[1:])


def finish(q_ref, refs, o_ref, peak_ref, total_ref, h):
    start = (peak_ref[h][:, :1], total_ref[h][:, :1], o_ref[:, h * HD : (h + 1) * HD])
    peak, total, summed = attend(q_ref, refs, start, h)
    return summed * (1.0 / total), peak / math.sqrt(HD) + jnp.log(total)


def sent_body(q_ref, a_ref, b_ref, c_ref, d_ref, o_ref, peak_ref, total_ref, out_ref):
    rows = q_ref.shape[0]
    both = []
    for h in range(2):
        o, lse = finish(q_ref, (a_ref, b_ref, c_ref, d_ref), o_ref, peak_ref, total_ref, h)
        out_ref[:rows, h * HD : (h + 1) * HD] = o.astype(BF)
        both.append(lse)
    lane = lax.broadcasted_iota(jnp.int32, (rows, HD), 1)
    rest = jnp.transpose(jnp.where(lane == 0, both[0], both[1]))[:16]
    at = lax.broadcasted_iota(jnp.int32, (16, rows), 0)
    tail = jnp.zeros((16, rows), F32)
    for i in range(3):
        piece = rest.astype(BF).astype(F32)
        for h in range(2):
            tail = jnp.where(at == 3 * h + i, piece[h : h + 1], tail)
        rest = rest - piece
    out_ref[rows:, :] = tail.astype(BF)


def kept_body(q_ref, a_ref, b_ref, c_ref, d_ref, o_ref, peak_ref, total_ref, out_ref, lse_ref):
    for h in range(2):
        o, lse = finish(q_ref, (a_ref, b_ref, c_ref, d_ref), o_ref, peak_ref, total_ref, h)
        out_ref[:, h * HD : (h + 1) * HD] = o
        lse_ref[h] = jnp.broadcast_to(lse, lse_ref.shape[1:])


def merge_body(own_ref, lse_ref, got_ref, out_ref):
    rows = own_ref.shape[0]
    tail = got_ref[rows:, :].astype(F32)
    at = lax.broadcasted_iota(jnp.int32, (HD, rows), 0)
    row = [
        tail[3 * h : 3 * h + 1] + tail[3 * h + 1 : 3 * h + 2] + tail[3 * h + 2 : 3 * h + 3]
        for h in range(2)
    ]
    turned = jnp.transpose(jnp.where(at == 0, row[0], row[1]))
    for h in range(2):
        theirs = turned[:, h : h + 1]
        ours = lse_ref[h][:, :1]
        top = jnp.maximum(ours, theirs)
        a, b = jnp.exp(ours - top), jnp.exp(theirs - top)
        inverse = 1.0 / (a + b)
        cols = slice(h * HD, (h + 1) * HD)
        merged = (a * inverse) * own_ref[:, cols] + (b * inverse) * got_ref[:rows, cols].astype(F32)
        out_ref[:, cols] = merged.astype(BF)


def out_body(mdl_ref, own_ref, other_ref, wa_ref, wb_ref, *refs):
    *out_refs, x = refs
    for s, chip in enumerate(slot_chips(mdl_ref[0], False)):
        for k in range(2):
            rows = pl.ds(pl.multiple_of(128 * k + 16 * chip, 16), 16)
            x[s * 32 + 16 * k : s * 32 + 16 * k + 16, :256] = own_ref[rows, :]
            x[s * 32 + 16 * k : s * 32 + 16 * k + 16, 256:] = other_ref[rows, :]
    for at in range(0, wa_ref.shape[1], 512):
        cols = slice(at, at + 512)
        r = jnp.dot(x[:, :256], wa_ref[:, cols], preferred_element_type=F32) + jnp.dot(
            x[:, 256:], wb_ref[:, cols], preferred_element_type=F32
        )
        for s, out_ref in enumerate(out_refs):
            out_ref[:, cols] = r[32 * s : 32 * s + 32].astype(BF)


def add_body(*refs):
    *in_refs, out_ref = refs
    out_ref[...] = sum(r[...].astype(F32) for r in in_refs).astype(BF)


def sum_body(core_ref, *refs):
    *in_refs, keep_ref, give_ref = refs
    k = core_ref[0]
    total = sum(r[...].astype(F32) for r in in_refs)
    keep_ref[...] = jnp.where(k == 0, total[:16], total[16:])
    give_ref[...] = jnp.where(k == 0, total[16:], total[:16])


def tail_body(
    core_ref, own_ref, other_ref, x_ref, gate_ref, scale_ref, wf_ref, state_ref, noise_ref,
    owner_ref, hidden_ref, next_ref, slot_ref, vel,
):
    k = core_ref[0]
    own, other = own_ref[...], other_ref[...]
    left = jnp.where(k == 0, own, other)
    right = jnp.where(k == 0, other, own)
    blocks, rows, width = x_ref.shape
    half = blocks // 2
    mixed = []
    square = jnp.zeros((rows, width), F32)
    for b in range(blocks):
        at = (b % half) * width
        part = (left if b < half else right)[:, at : at + width]
        mix = x_ref[b].astype(F32) + gate_ref[b : b + 1] * part
        hidden_ref[:, b * width : (b + 1) * width] = mix.astype(BF)
        square = square + mix * mix
        mixed.append(mix)
    inverse = lax.rsqrt(jnp.sum(square, -1, keepdims=True) / (blocks * width) + 1e-06)
    acc = jnp.zeros(vel.shape, F32)
    for b in range(blocks):
        normed = (mixed[b] * inverse * (1.0 + scale_ref[b : b + 1])).astype(BF)
        acc = acc + lax.dot_general(
            normed,
            wf_ref[:, b * width : (b + 1) * width],
            (((1,), (1,)), ((), ())),
            preferred_element_type=F32,
        )
    vel[...] = acc
    tiles = state_ref.shape[0]
    lat = acc.shape[1]
    velocity = jnp.concatenate(
        [vel[pl.ds(j, tiles, stride=rows // tiles), :] for j in range(rows // tiles)], -1
    )
    state = state_ref[...]
    new = (
        state
        + 0.2 * (velocity + 0.5 * (0.5 * velocity - state) / (1.0 - 0.5))
        + math.sqrt(0.2) * noise_ref[...]
    )
    next_ref[...] = new
    panels = new.astype(BF).astype(F32)
    at = lax.broadcasted_iota(jnp.int32, slot_ref.shape, 0)
    slots = jnp.zeros(slot_ref.shape, F32)
    for t in range(tiles):
        owner = owner_ref[t]
        before = jnp.int32(0)
        for e in range(t):
            before = before + jnp.where(owner_ref[e] == owner, 1, 0)
        slots = jnp.where(at == owner * CAP + before, panels[t : t + 1], slots)
    slot_ref[...] = slots.astype(BF)


def up_body(x_ref, w_ref, out_ref):
    y = jnp.dot(x_ref[...], w_ref[...], preferred_element_type=F32)
    out_ref[...] = jax.nn.gelu(y).astype(BF)


def shards(
    latents, mod_shift, mod_scale, gate, w_query, w_key, w_value, w_out, cache_keys,
    cache_values, final_scale, w_final, state, noise, owners, w_up,
):
    count, part = latents.shape
    mdl = lax.axis_index("mdl")
    core = mdl % 2
    core_1 = jnp.reshape(core, (1,)).astype(jnp.int32)
    mdl_1 = jnp.reshape(mdl, (1,)).astype(jnp.int32)
    chips = 8
    block = count // 16
    rows = count // 2

    cached = call(
        join_body,
        (shape((cache_keys.shape[0], 2 * cache_keys.shape[1]), BF),),
        (cache_keys, cache_values),
    )[0]
    far = lax.ppermute(cached, "ctx", x_step(2))
    keep, give = call(
        turn_body,
        (shape((rows, part), BF), shape((rows, part), BF)),
        (core_1, latents.T),
        smem=(0,),
    )
    got = core_swap(give)
    is_first = core == 0
    wide = jnp.concatenate(
        [jnp.where(is_first, keep, got), jnp.where(is_first, got, keep)], 1
    )
    beside = lax.ppermute(wide, "mdl", PAIR_SWAP)
    x = [wide, beside] + [z_send(a, by) for a in (wide, beside) for by in STEPS]

    near = [lax.ppermute(cached, "ctx", x_step(by)) for by in (1, 3)]

    half = w_out.shape[1] // 2
    w_mine, w_give = call(
        halves_body,
        (shape((w_out.shape[0], half), BF), shape((w_out.shape[0], half), BF)),
        (core_1, w_out),
        smem=(0,),
        after=(beside,),
    )
    w_theirs = core_swap(w_give)

    normed, own_x = call(
        norm_body,
        (shape((rows, chips * 2 * part), BF), shape((chips, block, 2 * part), BF)),
        (mdl_1, *x, mod_scale.reshape(chips, 2 * part), mod_shift.reshape(chips, 2 * part)),
        smem=(0,),
        flops=MIB,
        nbytes=MIB,
        after=(far, *near, w_mine),
    )
    cols = w_query.shape[1]
    weights = call(
        load_body,
        tuple(shape(w.shape, BF) for w in (w_query, w_key, w_value)),
        (w_query, w_key, w_value),
        hbm=(0, 1, 2),
        nbytes=8 * MIB,
        scratch=[pltpu.SemaphoreType.DMA((3, 4))],
        after=(normed,),
    )
    kv, whole = call(
        kv_body,
        (shape((count, 2 * cols), BF), shape((count, w_query.shape[0]), BF)),
        (core_1, normed, core_swap(normed), *weights[1:]),
        smem=(0,),
        flops=2 * count * w_query.shape[0] * 2 * cols,
        nbytes=8 * MIB,
    )
    query = call(
        query_body,
        shape((count, cols), BF),
        (whole, weights[0]),
        flops=2 * count * w_query.shape[0] * cols,
        nbytes=5 * MIB,
    )
    fresh = [kv] + [lax.ppermute(kv, "ctx", x_step(by)) for by in (1, 3, 2)]
    query_in = lax.ppermute(query, "ctx", Y_SWAP)

    def past_call(q, after=()):
        return call(
            past_body,
            (
                shape((count, cols), F32),
                shape((2, count, HD), F32),
                shape((2, count, HD), F32),
            ),
            (q, cached, far, *near),
            flops=4 * count * 2048 * 256,
            nbytes=4 * MIB,
            trans=count * 4096,
            after=after,
        )

    stats_own = past_call(query)
    stats_in = past_call(query_in, stats_own[:1])
    sent = call(
        sent_body,
        shape((count + 16, cols), BF),
        (query_in, *fresh, *stats_in),
        flops=4 * count * 1024 * 256,
        nbytes=2 * MIB,
        trans=count * 2048,
    )
    back = lax.ppermute(sent, "ctx", Y_SWAP)
    kept = call(
        kept_body,
        (shape((count, cols), F32), shape((2, count, HD), F32)),
        (query, *fresh, *stats_own),
        flops=4 * count * 1024 * 256,
        nbytes=2 * MIB,
        trans=count * 2048,
    )
    attended = call(merge_body, shape((count, cols), BF), (*kept, back), nbytes=MIB)

    projected = call(
        out_body,
        tuple(shape((2 * block, half), BF) for _ in range(chips)),
        (mdl_1, attended, core_swap(attended), w_mine, w_theirs),
        smem=(0,),
        flops=2 * count * 512 * half,
        nbytes=4 * MIB,
        scratch=[pltpu.VMEM((count, 2 * cols), BF)],
    )
    here, passing = projected[0], projected[1]
    relayed = [z_send(a, by) for a, by in zip(projected[5:], STEPS)]
    direct = [z_send(a, by) for a, by in zip(projected[2:5], STEPS)]
    passed = lax.ppermute(
        call(add_body, shape(passing.shape, BF), (passing, *relayed)), "mdl", PAIR_SWAP
    )
    ours, theirs = call(
        sum_body,
        (shape((block, half), F32), shape((block, half), F32)),
        (core_1, here, *direct, passed),
        smem=(0,),
        nbytes=2 * MIB,
    )
    hidden_out, next_state, slot_rows = call(
        tail_body,
        (
            shape((block, w_out.shape[1]), BF),
            shape(state.shape, F32),
            shape((16 * CAP, state.shape[1]), BF),
        ),
        (
            core_1, ours, core_swap(theirs), own_x, gate.reshape(chips, 2 * part),
            final_scale.reshape(chips, 2 * part), w_final.T, state, noise, owners[:, 0],
        ),
        smem=(0, 9),
        nbytes=2 * MIB,
        scratch=[pltpu.VMEM((block, w_final.shape[1]), F32)],
    )
    routed = lax.all_to_all(
        slot_rows.reshape(16, CAP, state.shape[1]), "mdl", split_axis=0, concat_axis=0, tiled=True
    ).reshape(16 * CAP, state.shape[1])
    upsampled = call(
        up_body, shape((16 * CAP, w_up.shape[1]), BF), (routed, w_up), nbytes=MIB
    )
    return (hidden_out, next_state, upsampled)


def solution(mesh):
    return jax.shard_map(
        shards,
        mesh=mesh,
        in_specs=(
            P("ctx", "mdl"),
            P(),
            P(),
            P(),
            P(None, "mdl"),
            P(None, "mdl"),
            P(None, "mdl"),
            P("mdl", None),
            P("ctx", "mdl"),
            P("ctx", "mdl"),
            P(),
            P(),
            P(("ctx", "mdl"), None),
            P(("ctx", "mdl"), None),
            P(("ctx", "mdl"), None),
            P(),
        ),
        out_specs=(P(("ctx", "mdl"), None), P(("ctx", "mdl"), None), P(("ctx", "mdl"), None)),
        check_vma=False,
    )
```

```python
import functools
import math

import jax
import jax.numpy as jnp
from jax import lax
from jax.experimental import pallas as pl
from jax.experimental.pallas import tpu as pltpu
from jax.sharding import PartitionSpec as P

HD = 128
CAP = 2
BF = jnp.bfloat16
F32 = jnp.float32
MIB = 1 << 20
VM = pl.BlockSpec(memory_space=pltpu.VMEM)
SM = pl.BlockSpec(memory_space=pltpu.SMEM)
HB = pl.BlockSpec(memory_space=pltpu.HBM)

CORE_SWAP = [(m, m ^ 1) for m in range(16)]
PAIR_SWAP = [(m, m ^ 2) for m in range(16)]
STEPS = (1, 3, 2)


def y_swap(a):
    return lax.ppermute(a, "ctx", [(c, c ^ 4) for c in range(8)])


def x_send(a, by):
    return lax.ppermute(a, "ctx", [(c, (c // 4) * 4 + (c + by) % 4) for c in range(8)])


def core_swap(a):
    return lax.ppermute(a, "mdl", CORE_SWAP)


def pair_swap(a):
    return lax.ppermute(a, "mdl", PAIR_SWAP)


def z_send(a, by):
    return lax.ppermute(a, "mdl", [(m, (m + 4 * by) % 16) for m in range(16)])


def slot_chips(mdl, back):
    z, h = mdl >> 2, (mdl >> 1) & 1
    around = [(z + (-by if back else by)) & 3 for by in STEPS]
    return [z * 2 + h, z * 2 + 1 - h] + [a * 2 + h for a in around] + [a * 2 + 1 - h for a in around]


def call(
    body, outs, args, flops=0, nbytes=0, trans=0, smem=(), hbm=(), scratch=(), limit=24, after=()
):
    count = len(args)
    place = [SM if i in smem else HB if i in hbm else VM for i in range(count)]

    def run(*refs):
        body(*refs[:count], *refs[count + len(after) :])

    return pl.pallas_call(
        run,
        out_shape=outs,
        in_specs=place
        + [pl.BlockSpec(memory_space=pl.ANY)] * len(after),
        out_specs=jax.tree.map(lambda o: VM, outs),
        scratch_shapes=list(scratch),
        compiler_params=pltpu.CompilerParams(vmem_limit_bytes=limit * MIB),
        cost_estimate=pl.CostEstimate(flops=flops, bytes_accessed=nbytes, transcendentals=trans),
    )(*args, *after)


def shape(dims, dtype):
    return jax.ShapeDtypeStruct(dims, dtype)


def turn_body(core_ref, x_ref, keep_ref, give_ref):
    k = core_ref[0]
    block = 16
    x = jnp.transpose(x_ref[...])
    for j in range(x.shape[0] // (2 * block)):
        first = x[2 * j * block : (2 * j + 1) * block]
        second = x[(2 * j + 1) * block : (2 * j + 2) * block]
        keep_ref[j * block : (j + 1) * block] = jnp.where(k == 0, first, second)
        give_ref[j * block : (j + 1) * block] = jnp.where(k == 0, second, first)


def copy_body(x_ref, out_ref):
    out_ref[...] = x_ref[...]


def join_body(a_ref, b_ref, out_ref, sems):
    width = a_ref.shape[1]
    copies = [
        pltpu.make_async_copy(ref, out_ref.at[:, pl.ds(i * width, width)], sems.at[i])
        for i, ref in enumerate((a_ref, b_ref))
    ]
    for copy in copies:
        copy.start()
    for copy in copies:
        copy.wait()


def load_body(*refs):
    *refs, sems = refs
    half = len(refs) // 2
    pieces = sems.shape[1]
    copies = []
    for i, (src, dst) in enumerate(zip(refs[:half], refs[half:])):
        some = src.shape[0] // pieces
        for j in range(pieces):
            rows = pl.ds(j * some, some)
            copies.append(pltpu.make_async_copy(src.at[rows], dst.at[rows], sems.at[i, j]))
    for copy in copies:
        copy.start()
    for copy in copies:
        copy.wait()


def halves_body(core_ref, w_ref, mine_ref, theirs_ref):
    k = core_ref[0]
    width = mine_ref.shape[1]
    mine_ref[...] = w_ref[:, pl.ds(pl.multiple_of(k * width, width), width)]
    theirs_ref[...] = w_ref[:, pl.ds(pl.multiple_of((1 - k) * width, width), width)]


def norm_body(mdl_ref, *refs):
    *x_refs, scale_ref, shift_ref, out_ref, own_ref = refs
    blocks = len(x_refs)
    rows, width = x_refs[0].shape
    total = sum(x_ref[...].astype(F32) for x_ref in x_refs)
    mean = jnp.sum(total, -1, keepdims=True) / (blocks * width)
    square = jnp.zeros((rows, width), F32)
    for x_ref in x_refs:
        centred = x_ref[...].astype(F32) - mean
        square = square + centred * centred
    var = jnp.sum(square, -1, keepdims=True) / (blocks * width)
    inverse = lax.rsqrt(var + 1e-06)
    chips = slot_chips(mdl_ref[0], True)
    block = own_ref.shape[1]
    here = pl.ds(pl.multiple_of(chips[0] * block, block), block)
    for chip, x_ref in zip(chips, x_refs):
        own_ref[chip] = x_ref[here, :]
        centred = x_ref[...].astype(F32) - mean
        scale, shift = scale_ref[pl.ds(chip, 1)], shift_ref[pl.ds(chip, 1)]
        cols = pl.ds(pl.multiple_of(chip * width, width), width)
        out_ref[:, cols] = (centred * inverse * (1.0 + scale) + shift).astype(BF)


def kv_body(core_ref, own_ref, other_ref, wk_ref, wv_ref, kv_ref, x):
    k = core_ref[0]
    rows = own_ref.shape[0]
    x[pl.ds(pl.multiple_of(k * rows, rows), rows), :] = own_ref[...]
    x[pl.ds(pl.multiple_of((1 - k) * rows, rows), rows), :] = other_ref[...]
    kv_ref[:, :256] = jnp.dot(x[...], wk_ref[...], preferred_element_type=F32).astype(BF)
    kv_ref[:, 256:] = jnp.dot(x[...], wv_ref[...], preferred_element_type=F32).astype(BF)


def query_body(x_ref, wq_ref, q_ref):
    q_ref[...] = jnp.dot(x_ref[...], wq_ref[...], preferred_element_type=F32).astype(BF)


C2 = math.log2(math.e) / math.sqrt(HD)


def fold(op, parts):
    return functools.reduce(
        op, [p[:, at : at + HD] for p in parts for at in range(0, p.shape[1], HD)]
    )


def attend(q_ref, kv_refs, start, h):
    q = q_ref[:, h * HD : (h + 1) * HD]
    scores = [
        lax.dot_general(
            q, kv[:, h * HD : (h + 1) * HD], (((1,), (1,)), ((), ())), preferred_element_type=F32
        )
        for kv in kv_refs
    ]
    peak = jnp.max(fold(jnp.maximum, scores), -1, keepdims=True)
    if start is not None:
        peak = jnp.maximum(peak, start[0])
    probs = [jnp.exp2((s - peak) * C2) for s in scores]
    total = jnp.sum(fold(jnp.add, probs), -1, keepdims=True)
    summed = sum(
        jnp.dot(
            p.astype(BF), kv[:, 256 + h * HD : 256 + (h + 1) * HD], preferred_element_type=F32
        )
        for p, kv in zip(probs, kv_refs)
    )
    if start is not None:
        factor = jnp.exp2((start[0] - peak) * C2)
        total, summed = start[1] * factor + total, start[2] * factor + summed
    return peak, total, summed


def past_body(q_ref, *refs):
    *kv_refs, o_ref, peak_ref, total_ref = refs
    for h in range(2):
        peak, total, summed = attend(q_ref, kv_refs, None, h)
        o_ref[:, h * HD : (h + 1) * HD] = summed
        peak_ref[h] = jnp.broadcast_to(peak, peak_ref.shape[1:])
        total_ref[h] = jnp.broadcast_to(total, total_ref.shape[1:])


def log_total(peak, total):
    return peak / math.sqrt(HD) + jnp.log(total)


def sent_body(q_ref, *refs):
    *kv_refs, out_ref = refs
    rows = q_ref.shape[0]
    both = []
    for h in range(2):
        peak, total, summed = attend(q_ref, kv_refs, None, h)
        out_ref[:rows, h * HD : (h + 1) * HD] = (summed * (1.0 / total)).astype(BF)
        both.append(log_total(peak, total))
    lane = lax.broadcasted_iota(jnp.int32, (rows, HD), 1)
    rest = jnp.transpose(jnp.where(lane == 0, both[0], both[1]))[:16]
    at = lax.broadcasted_iota(jnp.int32, (16, rows), 0)
    tail = jnp.zeros((16, rows), F32)
    for i in range(3):
        piece = rest.astype(BF).astype(F32)
        for h in range(2):
            tail = jnp.where(at == 3 * h + i, piece[h : h + 1], tail)
        rest = rest - piece
    out_ref[rows:, :] = tail.astype(BF)


def kept_body(q_ref, a_ref, b_ref, o_ref, peak_ref, total_ref, out_ref, lse_ref):
    for h in range(2):
        cols = slice(h * HD, (h + 1) * HD)
        start = (peak_ref[h][:, :1], total_ref[h][:, :1], o_ref[:, cols])
        peak, total, summed = attend(q_ref, (a_ref, b_ref), start, h)
        out_ref[:, cols] = summed * (1.0 / total)
        lse_ref[h] = jnp.broadcast_to(log_total(peak, total), lse_ref.shape[1:])


def merge_body(own_ref, lse_ref, *refs):
    *got_refs, out_ref = refs
    rows = own_ref.shape[0]
    at = lax.broadcasted_iota(jnp.int32, (HD, rows), 0)
    lanes = jnp.zeros((HD, rows), F32)
    for g, got_ref in enumerate(got_refs):
        tail = got_ref[rows:, :].astype(F32)
        for h in range(2):
            row = sum(tail[3 * h + i : 3 * h + i + 1] for i in range(3))
            lanes = jnp.where(at == 2 * g + h, row, lanes)
    turned = jnp.transpose(lanes)
    for h in range(2):
        cols = slice(h * HD, (h + 1) * HD)
        lse = [lse_ref[h][:, :1]] + [
            turned[:, 2 * g + h : 2 * g + h + 1] for g in range(len(got_refs))
        ]
        top = functools.reduce(jnp.maximum, lse)
        part = [jnp.exp(e - top) for e in lse]
        inverse = 1.0 / sum(part)
        merged = (part[0] * inverse) * own_ref[:, cols]
        for p, got_ref in zip(part[1:], got_refs):
            merged = merged + (p * inverse) * got_ref[:rows, cols].astype(F32)
        out_ref[:, cols] = merged.astype(BF)


def out_body(mdl_ref, own_ref, other_ref, wa_ref, wb_ref, *refs):
    *out_refs, x = refs
    for s, chip in enumerate(slot_chips(mdl_ref[0], False)):
        for k in range(2):
            rows = pl.ds(pl.multiple_of(128 * k + 16 * chip, 16), 16)
            x[s * 32 + 16 * k : s * 32 + 16 * k + 16, :256] = own_ref[rows, :]
            x[s * 32 + 16 * k : s * 32 + 16 * k + 16, 256:] = other_ref[rows, :]
    for at in range(0, wa_ref.shape[1], 512):
        cols = slice(at, at + 512)
        r = jnp.dot(x[:, :256], wa_ref[:, cols], preferred_element_type=F32) + jnp.dot(
            x[:, 256:], wb_ref[:, cols], preferred_element_type=F32
        )
        for s, out_ref in enumerate(out_refs):
            out_ref[:, cols] = r[32 * s : 32 * s + 32].astype(BF)


def add_body(*refs):
    *in_refs, out_ref = refs
    out_ref[...] = sum(r[...].astype(F32) for r in in_refs).astype(BF)


def sum_body(core_ref, *refs):
    *in_refs, keep_ref, give_ref = refs
    k = core_ref[0]
    total = sum(r[...].astype(F32) for r in in_refs)
    keep_ref[...] = jnp.where(k == 0, total[:16], total[16:])
    give_ref[...] = jnp.where(k == 0, total[16:], total[:16])


def tail_body(
    core_ref, own_ref, other_ref, x_ref, gate_ref, scale_ref, wf_ref, state_ref, noise_ref,
    owner_ref, hidden_ref, next_ref, slot_ref, vel,
):
    k = core_ref[0]
    own, other = own_ref[...], other_ref[...]
    left = jnp.where(k == 0, own, other)
    right = jnp.where(k == 0, other, own)
    blocks, rows, width = x_ref.shape
    half = blocks // 2
    mixed = []
    square = jnp.zeros((rows, width), F32)
    for b in range(blocks):
        at = (b % half) * width
        part = (left if b < half else right)[:, at : at + width]
        mix = x_ref[b].astype(F32) + gate_ref[b : b + 1] * part
        hidden_ref[:, b * width : (b + 1) * width] = mix.astype(BF)
        square = square + mix * mix
        mixed.append(mix)
    inverse = lax.rsqrt(jnp.sum(square, -1, keepdims=True) / (blocks * width) + 1e-06)
    acc = jnp.zeros(vel.shape, F32)
    for b in range(blocks):
        normed = (mixed[b] * inverse * (1.0 + scale_ref[b : b + 1])).astype(BF)
        acc = acc + lax.dot_general(
            normed,
            wf_ref[:, b * width : (b + 1) * width],
            (((1,), (1,)), ((), ())),
            preferred_element_type=F32,
        )
    vel[...] = acc
    tiles = state_ref.shape[0]
    lat = acc.shape[1]
    velocity = jnp.concatenate(
        [vel[pl.ds(j, tiles, stride=rows // tiles), :] for j in range(rows // tiles)], -1
    )
    state = state_ref[...]
    new = (
        state
        + 0.2 * (velocity + 0.5 * (0.5 * velocity - state) / (1.0 - 0.5))
        + math.sqrt(0.2) * noise_ref[...]
    )
    next_ref[...] = new
    panels = new.astype(BF).astype(F32)
    at = lax.broadcasted_iota(jnp.int32, slot_ref.shape, 0)
    slots = jnp.zeros(slot_ref.shape, F32)
    for t in range(tiles):
        owner = owner_ref[t]
        before = jnp.int32(0)
        for e in range(t):
            before = before + jnp.where(owner_ref[e] == owner, 1, 0)
        slots = jnp.where(at == owner * CAP + before, panels[t : t + 1], slots)
    slot_ref[...] = slots.astype(BF)


def up_body(x_ref, w_ref, out_ref):
    y = jnp.dot(x_ref[...], w_ref[...], preferred_element_type=F32)
    out_ref[...] = jax.nn.gelu(y).astype(BF)


def shards(
    latents, mod_shift, mod_scale, gate, w_query, w_key, w_value, w_out, cache_keys,
    cache_values, final_scale, w_final, state, noise, owners, w_up,
):
    count, part = latents.shape
    mdl = lax.axis_index("mdl")
    core = mdl % 2
    core_1 = jnp.reshape(core, (1,)).astype(jnp.int32)
    mdl_1 = jnp.reshape(mdl, (1,)).astype(jnp.int32)
    chips = 8
    block = count // 16
    rows = count // 2

    cached = call(
        join_body,
        shape((cache_keys.shape[0], 2 * cache_keys.shape[1]), BF),
        (cache_keys, cache_values),
        hbm=(0, 1),
        scratch=[pltpu.SemaphoreType.DMA((2,))],
    )
    keep, give = call(
        turn_body,
        (shape((rows, part), BF), shape((rows, part), BF)),
        (core_1, latents.T),
        smem=(0,),
    )
    got = core_swap(give)
    is_first = core == 0
    wide = jnp.concatenate(
        [jnp.where(is_first, keep, got), jnp.where(is_first, got, keep)], 1
    )
    beside = pair_swap(wide)
    mine = [z_send(wide, by) for by in STEPS]
    x = [wide, beside] + mine + [z_send(beside, by) for by in STEPS]

    cached_in = y_swap(call(copy_body, shape(cached.shape, BF), (cached,), after=(beside,)))

    half = w_out.shape[1] // 2
    w_mine, w_give = call(
        halves_body,
        (shape((w_out.shape[0], half), BF), shape((w_out.shape[0], half), BF)),
        (core_1, w_out),
        smem=(0,),
        after=(beside,),
    )
    w_theirs = core_swap(w_give)

    weights = call(
        load_body,
        tuple(shape(w.shape, BF) for w in (w_query, w_key, w_value)),
        (w_query, w_key, w_value),
        hbm=(0, 1, 2),
        nbytes=8 * MIB,
        scratch=[pltpu.SemaphoreType.DMA((3, 4))],
        limit=42,
        flops=5000000000,
        after=tuple(mine),
    )
    normed, own_x = call(
        norm_body,
        (shape((rows, chips * 2 * part), BF), shape((chips, block, 2 * part), BF)),
        (
            mdl_1, *x, mod_scale.reshape(chips, 2 * part), mod_shift.reshape(chips, 2 * part),
        ),
        smem=(0,),
        flops=MIB,
        nbytes=MIB,
        after=(cached_in, w_mine, *weights),
    )
    cols = w_query.shape[1]
    kv, whole = call(
        kv_body,
        (shape((count, 2 * cols), BF), shape((count, w_query.shape[0]), BF)),
        (core_1, normed, core_swap(normed), *weights[1:]),
        smem=(0,),
        flops=2 * count * w_query.shape[0] * 2 * cols,
        nbytes=8 * MIB,
    )
    query = call(
        query_body,
        shape((count, cols), BF),
        (whole, weights[0]),
        flops=2 * count * w_query.shape[0] * cols,
        nbytes=5 * MIB,
    )
    kv_in = y_swap(kv)
    query_in = [x_send(query, by) for by in STEPS]

    stats = call(
        past_body,
        (
            shape((count, cols), F32),
            shape((2, count, HD), F32),
            shape((2, count, HD), F32),
        ),
        (query, cached, cached_in),
        flops=MIB,
        nbytes=MIB,
    )
    back, before = [], stats[0]
    for by, q in zip(STEPS, query_in):
        before = call(
            sent_body,
            shape((count + 16, cols), BF),
            (q, cached, cached_in, kv, kv_in),
            flops=MIB,
            nbytes=MIB,
            after=(before,),
        )
        back.append(x_send(before, -by))
    kept = call(
        kept_body,
        (shape((count, cols), F32), shape((2, count, HD), F32)),
        (query, kv, kv_in, *stats),
        flops=MIB,
        nbytes=MIB,
        after=(before,),
    )
    attended = call(merge_body, shape((count, cols), BF), (*kept, *back), nbytes=MIB)

    projected = call(
        out_body,
        tuple(shape((2 * block, half), BF) for _ in range(chips)),
        (mdl_1, attended, core_swap(attended), w_mine, w_theirs),
        smem=(0,),
        flops=2 * count * 512 * half,
        nbytes=4 * MIB,
        scratch=[pltpu.VMEM((count, 2 * cols), BF)],
    )
    def added(*parts):
        return call(add_body, shape(parts[0].shape, BF), parts)

    across = pair_swap(projected[7])
    relayed = [z_send(projected[5], 1), z_send(projected[6], 3)]
    direct = [z_send(projected[2], 1), z_send(projected[3], 3)]
    direct.append(z_send(added(projected[4], across), 2))
    passed = pair_swap(added(projected[1], *relayed))
    ours, theirs = call(
        sum_body,
        (shape((block, half), F32), shape((block, half), F32)),
        (core_1, projected[0], *direct, passed),
        smem=(0,),
        nbytes=2 * MIB,
    )
    hidden_out, next_state, slot_rows = call(
        tail_body,
        (
            shape((block, w_out.shape[1]), BF),
            shape(state.shape, F32),
            shape((16 * CAP, state.shape[1]), BF),
        ),
        (
            core_1, ours, core_swap(theirs), own_x, gate.reshape(chips, 2 * part),
            final_scale.reshape(chips, 2 * part), w_final.T, state, noise, owners[:, 0],
        ),
        smem=(0, 9),
        nbytes=2 * MIB,
        scratch=[pltpu.VMEM((block, w_final.shape[1]), F32)],
    )
    routed = lax.all_to_all(
        slot_rows.reshape(16, CAP, state.shape[1]), "mdl", split_axis=0, concat_axis=0, tiled=True
    ).reshape(16 * CAP, state.shape[1])
    upsampled = call(
        up_body, shape((16 * CAP, w_up.shape[1]), BF), (routed, w_up), nbytes=MIB
    )
    return (hidden_out, next_state, upsampled)


def solution(mesh):
    return jax.shard_map(
        shards,
        mesh=mesh,
        in_specs=(
            P("ctx", "mdl"),
            P(),
            P(),
            P(),
            P(None, "mdl"),
            P(None, "mdl"),
            P(None, "mdl"),
            P("mdl", None),
            P("ctx", "mdl"),
            P("ctx", "mdl"),
            P(),
            P(),
            P(("ctx", "mdl"), None),
            P(("ctx", "mdl"), None),
            P(("ctx", "mdl"), None),
            P(),
        ),
        out_specs=(P(("ctx", "mdl"), None), P(("ctx", "mdl"), None), P(("ctx", "mdl"), None)),
        check_vma=False,
    )
```

```python
import functools
import math

import jax
import jax.numpy as jnp
from jax import lax
from jax.experimental import pallas as pl
from jax.experimental.pallas import tpu as pltpu
from jax.sharding import PartitionSpec as P

HD = 128
CAP = 2
BF = jnp.bfloat16
F32 = jnp.float32
MIB = 1 << 20
VM = pl.BlockSpec(memory_space=pltpu.VMEM)
SM = pl.BlockSpec(memory_space=pltpu.SMEM)
HB = pl.BlockSpec(memory_space=pltpu.HBM)

CORE_SWAP = [(m, m ^ 1) for m in range(16)]
PAIR_SWAP = [(m, m ^ 2) for m in range(16)]
STEPS = (1, 3, 2)


def y_swap(a):
    return lax.ppermute(a, "ctx", [(c, c ^ 4) for c in range(8)])


def x_send(a, by):
    return lax.ppermute(a, "ctx", [(c, (c // 4) * 4 + (c + by) % 4) for c in range(8)])


def core_swap(a):
    return lax.ppermute(a, "mdl", CORE_SWAP)


def pair_swap(a):
    return lax.ppermute(a, "mdl", PAIR_SWAP)


def z_send(a, by):
    return lax.ppermute(a, "mdl", [(m, (m + 4 * by) % 16) for m in range(16)])


def slot_chips(mdl, back):
    z, h = mdl >> 2, (mdl >> 1) & 1
    around = [(z + (-by if back else by)) & 3 for by in STEPS]
    return [z * 2 + h, z * 2 + 1 - h] + [a * 2 + h for a in around] + [a * 2 + 1 - h for a in around]


def call(
    body, outs, args, flops=0, nbytes=0, trans=0, smem=(), hbm=(), scratch=(), limit=24, after=()
):
    count = len(args)
    place = [SM if i in smem else HB if i in hbm else VM for i in range(count)]

    def run(*refs):
        body(*refs[:count], *refs[count + len(after) :])

    return pl.pallas_call(
        run,
        out_shape=outs,
        in_specs=place
        + [pl.BlockSpec(memory_space=pl.ANY)] * len(after),
        out_specs=jax.tree.map(lambda o: VM, outs),
        scratch_shapes=list(scratch),
        compiler_params=pltpu.CompilerParams(vmem_limit_bytes=limit * MIB),
        cost_estimate=pl.CostEstimate(flops=flops, bytes_accessed=nbytes, transcendentals=trans),
    )(*args, *after)


def shape(dims, dtype):
    return jax.ShapeDtypeStruct(dims, dtype)


def turn_body(core_ref, x_ref, keep_ref, give_ref):
    k = core_ref[0]
    block = 16
    x = jnp.transpose(x_ref[...])
    for j in range(x.shape[0] // (2 * block)):
        first = x[2 * j * block : (2 * j + 1) * block]
        second = x[(2 * j + 1) * block : (2 * j + 2) * block]
        keep_ref[j * block : (j + 1) * block] = jnp.where(k == 0, first, second)
        give_ref[j * block : (j + 1) * block] = jnp.where(k == 0, second, first)


def copy_body(x_ref, out_ref):
    out_ref[...] = x_ref[...]


def join_body(a_ref, b_ref, out_ref, sems):
    width = a_ref.shape[1]
    copies = [
        pltpu.make_async_copy(ref, out_ref.at[:, pl.ds(i * width, width)], sems.at[i])
        for i, ref in enumerate((a_ref, b_ref))
    ]
    for copy in copies:
        copy.start()
    for copy in copies:
        copy.wait()


def load_body(*refs):
    *refs, sems = refs
    half = len(refs) // 2
    pieces = sems.shape[1]
    copies = []
    for i, (src, dst) in enumerate(zip(refs[:half], refs[half:])):
        some = src.shape[0] // pieces
        for j in range(pieces):
            rows = pl.ds(j * some, some)
            copies.append(pltpu.make_async_copy(src.at[rows], dst.at[rows], sems.at[i, j]))
    for copy in copies:
        copy.start()
    for copy in copies:
        copy.wait()


def halves_body(core_ref, w_ref, mine_ref, theirs_ref):
    k = core_ref[0]
    width = mine_ref.shape[1]
    mine_ref[...] = w_ref[:, pl.ds(pl.multiple_of(k * width, width), width)]
    theirs_ref[...] = w_ref[:, pl.ds(pl.multiple_of((1 - k) * width, width), width)]


def norm_body(mdl_ref, *refs):
    *x_refs, scale_ref, shift_ref, out_ref, own_ref = refs
    blocks = len(x_refs)
    rows, width = x_refs[0].shape
    total = sum(x_ref[...].astype(F32) for x_ref in x_refs)
    mean = jnp.sum(total, -1, keepdims=True) / (blocks * width)
    square = jnp.zeros((rows, width), F32)
    for x_ref in x_refs:
        centred = x_ref[...].astype(F32) - mean
        square = square + centred * centred
    var = jnp.sum(square, -1, keepdims=True) / (blocks * width)
    inverse = lax.rsqrt(var + 1e-06)
    chips = slot_chips(mdl_ref[0], True)
    block = own_ref.shape[1]
    here = pl.ds(pl.multiple_of(chips[0] * block, block), block)
    for chip, x_ref in zip(chips, x_refs):
        own_ref[chip] = x_ref[here, :]
        centred = x_ref[...].astype(F32) - mean
        scale, shift = scale_ref[pl.ds(chip, 1)], shift_ref[pl.ds(chip, 1)]
        cols = pl.ds(pl.multiple_of(chip * width, width), width)
        out_ref[:, cols] = (centred * inverse * (1.0 + scale) + shift).astype(BF)


def half_body(x_ref, wk_ref, wv_ref, wq_ref, kv_ref, q_ref):
    kv_ref[:, :256] = jnp.dot(x_ref[...], wk_ref[...], preferred_element_type=F32).astype(BF)
    kv_ref[:, 256:] = jnp.dot(x_ref[...], wv_ref[...], preferred_element_type=F32).astype(BF)
    q_ref[...] = jnp.dot(x_ref[...], wq_ref[...], preferred_element_type=F32).astype(BF)


def kv_body(x_ref, wk_ref, wv_ref, half_ref, kv_ref):
    rows = x_ref.shape[0]
    kv_ref[:rows] = half_ref[...]
    kv_ref[rows:, :256] = jnp.dot(x_ref[...], wk_ref[...], preferred_element_type=F32).astype(BF)
    kv_ref[rows:, 256:] = jnp.dot(x_ref[...], wv_ref[...], preferred_element_type=F32).astype(BF)


def query_body(core_ref, x_ref, wq_ref, half_ref, q_ref):
    k = core_ref[0]
    rows = x_ref.shape[0]
    q_ref[pl.ds(pl.multiple_of(k * rows, rows), rows), :] = half_ref[...]
    q_ref[pl.ds(pl.multiple_of((1 - k) * rows, rows), rows), :] = jnp.dot(
        x_ref[...], wq_ref[...], preferred_element_type=F32
    ).astype(BF)


C2 = math.log2(math.e) / math.sqrt(HD)


def fold(op, parts):
    return functools.reduce(
        op, [p[:, at : at + HD] for p in parts for at in range(0, p.shape[1], HD)]
    )


def attend(q_ref, kv_refs, which=(0, 1), starts=None):
    heads = [slice(h * HD, (h + 1) * HD) for h in which]
    every = [
        [
            lax.dot_general(
                q_ref[:, cols], kv[:, cols], (((1,), (1,)), ((), ())), preferred_element_type=F32
            )
            for kv in kv_refs
        ]
        for cols in heads
    ]
    results = []
    for h, scores in zip(which, every):
        peak = jnp.max(fold(jnp.maximum, scores), -1, keepdims=True)
        if starts is not None:
            peak = jnp.maximum(peak, starts[h][0])
        probs = [jnp.exp2((s - peak) * C2) for s in scores]
        total = jnp.sum(fold(jnp.add, probs), -1, keepdims=True)
        summed = sum(
            jnp.dot(
                p.astype(BF),
                kv[:, 256 + h * HD : 256 + (h + 1) * HD],
                preferred_element_type=F32,
            )
            for p, kv in zip(probs, kv_refs)
        )
        if starts is not None:
            factor = jnp.exp2((starts[h][0] - peak) * C2)
            total, summed = starts[h][1] * factor + total, starts[h][2] * factor + summed
        results.append((peak, total, summed))
    return results


def past_body(q_ref, *refs):
    *kv_refs, o_ref, peak_ref, total_ref = refs
    for h, (peak, total, summed) in enumerate(attend(q_ref, kv_refs)):
        o_ref[:, h * HD : (h + 1) * HD] = summed
        peak_ref[h] = jnp.broadcast_to(peak, peak_ref.shape[1:])
        total_ref[h] = jnp.broadcast_to(total, total_ref.shape[1:])


def log_total(peak, total):
    return peak / math.sqrt(HD) + jnp.log(total)


def turned(first, second):
    lane = lax.broadcasted_iota(jnp.int32, (first.shape[0], HD), 1)
    return jnp.transpose(jnp.where(lane == 0, first, second))[:8]


def sent_body(q_ref, *refs):
    *kv_refs, out_ref = refs
    rows = q_ref.shape[0]
    both = []
    for h, (peak, total, summed) in enumerate(attend(q_ref, kv_refs)):
        out_ref[:rows, h * HD : (h + 1) * HD] = (summed * (1.0 / total)).astype(BF)
        both.append(log_total(peak, total))
    rest = turned(*both)
    at = lax.broadcasted_iota(jnp.int32, (16, rows), 0)
    tail = jnp.zeros((16, rows), F32)
    for i in range(3):
        piece = rest.astype(BF).astype(F32)
        for h in range(2):
            tail = jnp.where(at == 3 * h + i, piece[h : h + 1], tail)
        rest = rest - piece
    out_ref[rows:, :] = tail.astype(BF)


def kept_body(q_ref, a_ref, b_ref, o_ref, peak_ref, total_ref, out_ref, lse_ref):
    both = []
    starts = [
        (peak_ref[h][:, :1], total_ref[h][:, :1], o_ref[:, h * HD : (h + 1) * HD]) for h in range(2)
    ]
    for h in range(2):
        peak, total, summed = attend(q_ref, (a_ref, b_ref), (h,), starts)[0]
        out_ref[:, h * HD : (h + 1) * HD] = summed * (1.0 / total)
        both.append(log_total(peak, total))
    lse_ref[...] = turned(*both)


def merge_body(own_ref, lse_ref, *refs):
    *got_refs, out_ref = refs
    rows = own_ref.shape[0]
    parts = len(got_refs) + 1
    at = lax.broadcasted_iota(jnp.int32, (HD, rows), 0)
    lanes = jnp.zeros((HD, rows), F32)
    tails = [got_ref[rows:, :].astype(F32) for got_ref in got_refs]
    for h in range(2):
        lse = [lse_ref[h : h + 1]] + [
            sum(tail[3 * h + i : 3 * h + i + 1] for i in range(3)) for tail in tails
        ]
        top = functools.reduce(jnp.maximum, lse)
        part = [jnp.exp(e - top) for e in lse]
        inverse = 1.0 / sum(part)
        for g, p in enumerate(part):
            lanes = jnp.where(at == parts * h + g, p * inverse, lanes)
    shares = jnp.transpose(lanes)
    for h in range(2):
        cols = slice(h * HD, (h + 1) * HD)
        merged = shares[:, parts * h : parts * h + 1] * own_ref[:, cols]
        for g, got_ref in enumerate(got_refs):
            share = shares[:, parts * h + g + 1 : parts * h + g + 2]
            merged = merged + share * got_ref[:rows, cols].astype(F32)
        out_ref[:, cols] = merged.astype(BF)


def out_body(mdl_ref, own_ref, other_ref, wa_ref, wb_ref, *refs):
    *out_refs, x = refs
    for s, chip in enumerate(slot_chips(mdl_ref[0], False)):
        for k in range(2):
            rows = pl.ds(pl.multiple_of(128 * k + 16 * chip, 16), 16)
            x[s * 32 + 16 * k : s * 32 + 16 * k + 16, :256] = own_ref[rows, :]
            x[s * 32 + 16 * k : s * 32 + 16 * k + 16, 256:] = other_ref[rows, :]
    for at in range(0, wa_ref.shape[1], 512):
        cols = slice(at, at + 512)
        r = jnp.dot(x[:, :256], wa_ref[:, cols], preferred_element_type=F32) + jnp.dot(
            x[:, 256:], wb_ref[:, cols], preferred_element_type=F32
        )
        for s, out_ref in enumerate(out_refs):
            out_ref[:, cols] = r[32 * s : 32 * s + 32].astype(BF)


def add_body(*refs):
    *in_refs, out_ref = refs
    out_ref[...] = sum(r[...].astype(F32) for r in in_refs).astype(BF)


def sum_body(core_ref, *refs):
    *in_refs, keep_ref, give_ref = refs
    k = core_ref[0]
    total = sum(r[...].astype(F32) for r in in_refs)
    keep_ref[...] = jnp.where(k == 0, total[:16], total[16:])
    give_ref[...] = jnp.where(k == 0, total[16:], total[:16])


def tail_body(
    core_ref, own_ref, other_ref, x_ref, gate_ref, scale_ref, wf_ref, state_ref, noise_ref,
    owner_ref, hidden_ref, next_ref, slot_ref, vel,
):
    k = core_ref[0]
    own, other = own_ref[...], other_ref[...]
    left = jnp.where(k == 0, own, other)
    right = jnp.where(k == 0, other, own)
    blocks, rows, width = x_ref.shape
    half = blocks // 2
    mixed = []
    square = jnp.zeros((rows, width), F32)
    for b in range(blocks):
        at = (b % half) * width
        part = (left if b < half else right)[:, at : at + width]
        mix = x_ref[b].astype(F32) + gate_ref[b : b + 1] * part
        hidden_ref[:, b * width : (b + 1) * width] = mix.astype(BF)
        square = square + mix * mix
        mixed.append(mix)
    inverse = lax.rsqrt(jnp.sum(square, -1, keepdims=True) / (blocks * width) + 1e-06)
    acc = jnp.zeros(vel.shape, F32)
    for b in range(blocks):
        normed = (mixed[b] * inverse * (1.0 + scale_ref[b : b + 1])).astype(BF)
        acc = acc + lax.dot_general(
            normed,
            wf_ref[:, b * width : (b + 1) * width],
            (((1,), (1,)), ((), ())),
            preferred_element_type=F32,
        )
    vel[...] = acc
    tiles = state_ref.shape[0]
    lat = acc.shape[1]
    velocity = jnp.concatenate(
        [vel[pl.ds(j, tiles, stride=rows // tiles), :] for j in range(rows // tiles)], -1
    )
    state = state_ref[...]
    new = (
        state
        + 0.2 * (velocity + 0.5 * (0.5 * velocity - state) / (1.0 - 0.5))
        + math.sqrt(0.2) * noise_ref[...]
    )
    next_ref[...] = new
    panels = new.astype(BF).astype(F32)
    owned = slot_ref.shape[0] * CAP
    at = lax.broadcasted_iota(jnp.int32, (owned, panels.shape[1]), 0)
    slots = jnp.zeros(at.shape, F32)
    for t in range(tiles):
        owner = owner_ref[t]
        before = jnp.int32(0)
        for e in range(t):
            before = before + jnp.where(owner_ref[e] == owner, 1, 0)
        slots = jnp.where(at == owner * CAP + before, panels[t : t + 1], slots)
    for o in range(slot_ref.shape[0]):
        slot_ref[o] = slots[CAP * o : CAP * o + CAP]


def up_body(x_ref, w_ref, out_ref):
    x = jnp.concatenate([x_ref[o] for o in range(x_ref.shape[0])], 0).astype(BF)
    y = jnp.dot(x, w_ref[...], preferred_element_type=F32)
    out_ref[...] = jax.nn.gelu(y).astype(BF)


def shards(
    latents, mod_shift, mod_scale, gate, w_query, w_key, w_value, w_out, cache_keys,
    cache_values, final_scale, w_final, state, noise, owners, w_up,
):
    count, part = latents.shape
    mdl = lax.axis_index("mdl")
    core = mdl % 2
    core_1 = jnp.reshape(core, (1,)).astype(jnp.int32)
    mdl_1 = jnp.reshape(mdl, (1,)).astype(jnp.int32)
    chips = 8
    block = count // 16
    rows = count // 2

    cached = call(
        join_body,
        shape((cache_keys.shape[0], 2 * cache_keys.shape[1]), BF),
        (cache_keys, cache_values),
        hbm=(0, 1),
        scratch=[pltpu.SemaphoreType.DMA((2,))],
    )
    keep, give = call(
        turn_body,
        (shape((rows, part), BF), shape((rows, part), BF)),
        (core_1, latents.T),
        smem=(0,),
    )
    got = core_swap(give)
    is_first = core == 0
    wide = jnp.concatenate(
        [jnp.where(is_first, keep, got), jnp.where(is_first, got, keep)], 1
    )
    beside = pair_swap(wide)
    mine = [z_send(wide, by) for by in STEPS]
    x = [wide, beside] + mine + [z_send(beside, by) for by in STEPS]

    cached_in = y_swap(call(copy_body, shape(cached.shape, BF), (cached,), after=(beside,)))

    half = w_out.shape[1] // 2
    w_mine, w_give = call(
        halves_body,
        (shape((w_out.shape[0], half), BF), shape((w_out.shape[0], half), BF)),
        (core_1, w_out),
        smem=(0,),
        after=(x[5],),
    )
    w_theirs = core_swap(w_give)

    weights = call(
        load_body,
        tuple(shape(w.shape, BF) for w in (w_query, w_key, w_value)),
        (w_query, w_key, w_value),
        hbm=(0, 1, 2),
        nbytes=8 * MIB,
        scratch=[pltpu.SemaphoreType.DMA((3, 4))],
        limit=45,
        flops=5000000000,
        after=tuple(mine),
    )
    normed, own_x = call(
        norm_body,
        (shape((rows, chips * 2 * part), BF), shape((chips, block, 2 * part), BF)),
        (
            mdl_1, *x, mod_scale.reshape(chips, 2 * part), mod_shift.reshape(chips, 2 * part),
        ),
        smem=(0,),
        flops=MIB,
        nbytes=MIB,
        after=(w_mine, *weights),
    )
    cols = w_query.shape[1]
    normed_in = core_swap(normed)
    kv_half, query_half = call(
        half_body,
        (shape((rows, 2 * cols), BF), shape((rows, cols), BF)),
        (normed, weights[1], weights[2], weights[0]),
        after=(cached_in,),
        flops=30000000000,
        nbytes=8 * MIB,
    )
    kv = call(
        kv_body,
        shape((count, 2 * cols), BF),
        (normed_in, weights[1], weights[2], kv_half),
        flops=2 * rows * w_query.shape[0] * 2 * cols,
        nbytes=5 * MIB,
    )
    query = call(
        query_body,
        shape((count, cols), BF),
        (core_1, normed_in, weights[0], query_half),
        smem=(0,),
        flops=2 * rows * w_query.shape[0] * cols,
        nbytes=3 * MIB,
    )
    kv_in = y_swap(kv)
    query_in = [x_send(query, by) for by in STEPS]

    stats = call(
        past_body,
        (
            shape((count, cols), F32),
            shape((2, count, HD), F32),
            shape((2, count, HD), F32),
        ),
        (query, cached, cached_in),
        flops=MIB,
        nbytes=MIB,
    )
    back, before = [], stats[0]
    for by, q in zip(STEPS, query_in):
        before = call(
            sent_body,
            shape((count + 16, cols), BF),
            (q, cached, cached_in, kv, kv_in),
            flops=MIB,
            nbytes=MIB,
            after=(before,),
        )
        back.append(x_send(before, -by))
    kept = call(
        kept_body,
        (shape((count, cols), F32), shape((8, count), F32)),
        (query, kv, kv_in, *stats),
        flops=MIB,
        nbytes=MIB,
        after=(before,),
    )
    attended = call(merge_body, shape((count, cols), BF), (*kept, *back), nbytes=MIB)

    projected = call(
        out_body,
        tuple(shape((2 * block, half), BF) for _ in range(chips)),
        (mdl_1, attended, core_swap(attended), w_mine, w_theirs),
        smem=(0,),
        flops=2 * count * 512 * half,
        nbytes=4 * MIB,
        scratch=[pltpu.VMEM((count, 2 * cols), BF)],
    )
    def added(*parts):
        return call(add_body, shape(parts[0].shape, BF), parts)

    across = pair_swap(projected[7])
    relayed = [z_send(projected[5], 1), z_send(projected[6], 3)]
    direct = [z_send(projected[2], 1), z_send(projected[3], 3)]
    direct.append(z_send(added(projected[4], across), 2))
    passed = pair_swap(added(projected[1], *relayed))
    ours, theirs = call(
        sum_body,
        (shape((block, half), F32), shape((block, half), F32)),
        (core_1, projected[0], *direct, passed),
        smem=(0,),
        nbytes=2 * MIB,
    )
    hidden_out, next_state, slot_rows = call(
        tail_body,
        (
            shape((block, w_out.shape[1]), BF),
            shape(state.shape, F32),
            shape((16, CAP, state.shape[1]), F32),
        ),
        (
            core_1, ours, core_swap(theirs), own_x, gate.reshape(chips, 2 * part),
            final_scale.reshape(chips, 2 * part), w_final.T, state, noise, owners[:, 0],
        ),
        smem=(0, 9),
        nbytes=2 * MIB,
        scratch=[pltpu.VMEM((block, w_final.shape[1]), F32)],
    )
    routed = lax.all_to_all(slot_rows, "mdl", split_axis=0, concat_axis=0, tiled=True)
    upsampled = call(
        up_body, shape((16 * CAP, w_up.shape[1]), BF), (routed, w_up), nbytes=MIB
    )
    return (hidden_out, next_state, upsampled)


def solution(mesh):
    return jax.shard_map(
        shards,
        mesh=mesh,
        in_specs=(
            P("ctx", "mdl"),
            P(),
            P(),
            P(),
            P(None, "mdl"),
            P(None, "mdl"),
            P(None, "mdl"),
            P("mdl", None),
            P("ctx", "mdl"),
            P("ctx", "mdl"),
            P(),
            P(),
            P(("ctx", "mdl"), None),
            P(("ctx", "mdl"), None),
            P(("ctx", "mdl"), None),
            P(),
        ),
        out_specs=(P(("ctx", "mdl"), None), P(("ctx", "mdl"), None), P(("ctx", "mdl"), None)),
        check_vma=False,
    )
```

```python
import functools
import math

import jax
import jax.numpy as jnp
from jax import lax
from jax.experimental import pallas as pl
from jax.experimental.pallas import tpu as pltpu
from jax.sharding import PartitionSpec as P

HD = 128
CAP = 2
BF = jnp.bfloat16
F32 = jnp.float32
MIB = 1 << 20
VM = pl.BlockSpec(memory_space=pltpu.VMEM)
SM = pl.BlockSpec(memory_space=pltpu.SMEM)
HB = pl.BlockSpec(memory_space=pltpu.HBM)

CORE_SWAP = [(m, m ^ 1) for m in range(16)]
PAIR_SWAP = [(m, m ^ 2) for m in range(16)]
STEPS = (1, 3, 2)


def y_swap(a):
    return lax.ppermute(a, "ctx", [(c, c ^ 4) for c in range(8)])


def x_send(a, by):
    return lax.ppermute(a, "ctx", [(c, (c // 4) * 4 + (c + by) % 4) for c in range(8)])


def core_swap(a):
    return lax.ppermute(a, "mdl", CORE_SWAP)


def pair_swap(a):
    return lax.ppermute(a, "mdl", PAIR_SWAP)


def z_send(a, by):
    return lax.ppermute(a, "mdl", [(m, (m + 4 * by) % 16) for m in range(16)])


def slot_chips(mdl, back):
    z, h = mdl >> 2, (mdl >> 1) & 1
    around = [(z + (-by if back else by)) & 3 for by in STEPS]
    return [z * 2 + h, z * 2 + 1 - h] + [a * 2 + h for a in around] + [a * 2 + 1 - h for a in around]


def call(
    body, outs, args, flops=0, nbytes=0, trans=0, smem=(), hbm=(), scratch=(), limit=24, after=()
):
    count = len(args)
    place = [SM if i in smem else HB if i in hbm else VM for i in range(count)]

    def run(*refs):
        body(*refs[:count], *refs[count + len(after) :])

    return pl.pallas_call(
        run,
        out_shape=outs,
        in_specs=place
        + [pl.BlockSpec(memory_space=pl.ANY)] * len(after),
        out_specs=jax.tree.map(lambda o: VM, outs),
        scratch_shapes=list(scratch),
        compiler_params=pltpu.CompilerParams(vmem_limit_bytes=limit * MIB),
        cost_estimate=pl.CostEstimate(flops=flops, bytes_accessed=nbytes, transcendentals=trans),
    )(*args, *after)


def shape(dims, dtype):
    return jax.ShapeDtypeStruct(dims, dtype)


def turn_body(core_ref, x_ref, keep_ref, give_ref):
    k = core_ref[0]
    block = 16
    x = jnp.transpose(x_ref[...])
    for j in range(x.shape[0] // (2 * block)):
        first = x[2 * j * block : (2 * j + 1) * block]
        second = x[(2 * j + 1) * block : (2 * j + 2) * block]
        keep_ref[j * block : (j + 1) * block] = jnp.where(k == 0, first, second)
        give_ref[j * block : (j + 1) * block] = jnp.where(k == 0, second, first)


def copy_body(x_ref, out_ref):
    out_ref[...] = x_ref[...]


def join_body(a_ref, b_ref, out_ref, sems):
    width = a_ref.shape[1]
    copies = [
        pltpu.make_async_copy(ref, out_ref.at[:, pl.ds(i * width, width)], sems.at[i])
        for i, ref in enumerate((a_ref, b_ref))
    ]
    for copy in copies:
        copy.start()
    for copy in copies:
        copy.wait()


def load_body(*refs):
    *refs, sems = refs
    half = len(refs) // 2
    pieces = sems.shape[1]
    copies = []
    for i, (src, dst) in enumerate(zip(refs[:half], refs[half:])):
        some = src.shape[0] // pieces
        for j in range(pieces):
            rows = pl.ds(j * some, some)
            copies.append(pltpu.make_async_copy(src.at[rows], dst.at[rows], sems.at[i, j]))
    for copy in copies:
        copy.start()
    for copy in copies:
        copy.wait()


def halves_body(core_ref, w_ref, mine_ref, theirs_ref):
    k = core_ref[0]
    width = mine_ref.shape[1]
    mine_ref[...] = w_ref[:, pl.ds(pl.multiple_of(k * width, width), width)]
    theirs_ref[...] = w_ref[:, pl.ds(pl.multiple_of((1 - k) * width, width), width)]


def norm_body(mdl_ref, *refs):
    *x_refs, scale_ref, shift_ref, out_ref, own_ref = refs
    blocks = len(x_refs)
    rows, width = x_refs[0].shape
    total = sum(x_ref[...].astype(F32) for x_ref in x_refs)
    mean = jnp.sum(total, -1, keepdims=True) / (blocks * width)
    square = jnp.zeros((rows, width), F32)
    for x_ref in x_refs:
        centred = x_ref[...].astype(F32) - mean
        square = square + centred * centred
    var = jnp.sum(square, -1, keepdims=True) / (blocks * width)
    inverse = lax.rsqrt(var + 1e-06)
    chips = slot_chips(mdl_ref[0], True)
    block = own_ref.shape[1]
    here = pl.ds(pl.multiple_of(chips[0] * block, block), block)
    for chip, x_ref in zip(chips, x_refs):
        own_ref[chip] = x_ref[here, :]
        centred = x_ref[...].astype(F32) - mean
        scale, shift = scale_ref[pl.ds(chip, 1)], shift_ref[pl.ds(chip, 1)]
        cols = pl.ds(pl.multiple_of(chip * width, width), width)
        out_ref[:, cols] = (centred * inverse * (1.0 + scale) + shift).astype(BF)


def half_body(x_ref, wk_ref, wv_ref, wq_ref, kv_ref, q_ref):
    kv_ref[:, :256] = jnp.dot(x_ref[...], wk_ref[...], preferred_element_type=F32).astype(BF)
    kv_ref[:, 256:] = jnp.dot(x_ref[...], wv_ref[...], preferred_element_type=F32).astype(BF)
    q_ref[...] = jnp.dot(x_ref[...], wq_ref[...], preferred_element_type=F32).astype(BF)


def kv_body(x_ref, wk_ref, wv_ref, kv_ref):
    kv_ref[:, :256] = jnp.dot(x_ref[...], wk_ref[...], preferred_element_type=F32).astype(BF)
    kv_ref[:, 256:] = jnp.dot(x_ref[...], wv_ref[...], preferred_element_type=F32).astype(BF)


def query_body(core_ref, x_ref, wq_ref, half_ref, q_ref):
    k = core_ref[0]
    rows = x_ref.shape[0]
    q_ref[pl.ds(pl.multiple_of(k * rows, rows), rows), :] = half_ref[...]
    q_ref[pl.ds(pl.multiple_of((1 - k) * rows, rows), rows), :] = jnp.dot(
        x_ref[...], wq_ref[...], preferred_element_type=F32
    ).astype(BF)


C2 = math.log2(math.e) / math.sqrt(HD)


def fold(op, parts):
    return functools.reduce(
        op, [p[:, at : at + HD] for p in parts for at in range(0, p.shape[1], HD)]
    )


def attend(q_ref, kv_refs, which=(0, 1), starts=None):
    heads = [slice(h * HD, (h + 1) * HD) for h in which]
    every = [
        [
            lax.dot_general(
                q_ref[:, cols], kv[:, cols], (((1,), (1,)), ((), ())), preferred_element_type=F32
            )
            for kv in kv_refs
        ]
        for cols in heads
    ]
    results = []
    for h, scores in zip(which, every):
        peak = jnp.max(fold(jnp.maximum, scores), -1, keepdims=True)
        if starts is not None:
            peak = jnp.maximum(peak, starts[h][0])
        probs = [jnp.exp2((s - peak) * C2) for s in scores]
        total = jnp.sum(fold(jnp.add, probs), -1, keepdims=True)
        summed = sum(
            jnp.dot(
                p.astype(BF),
                kv[:, 256 + h * HD : 256 + (h + 1) * HD],
                preferred_element_type=F32,
            )
            for p, kv in zip(probs, kv_refs)
        )
        if starts is not None:
            factor = jnp.exp2((starts[h][0] - peak) * C2)
            total, summed = starts[h][1] * factor + total, starts[h][2] * factor + summed
        results.append((peak, total, summed))
    return results


def past_body(q_ref, *refs):
    *kv_refs, o_ref, peak_ref, total_ref = refs
    for h, (peak, total, summed) in enumerate(attend(q_ref, kv_refs)):
        o_ref[:, h * HD : (h + 1) * HD] = summed
        peak_ref[h] = jnp.broadcast_to(peak, peak_ref.shape[1:])
        total_ref[h] = jnp.broadcast_to(total, total_ref.shape[1:])


def log_total(peak, total):
    return peak / math.sqrt(HD) + jnp.log(total)


def turned(first, second):
    lane = lax.broadcasted_iota(jnp.int32, (first.shape[0], HD), 1)
    return jnp.transpose(jnp.where(lane == 0, first, second))[:8]


def sent_body(q_ref, *refs):
    *kv_refs, out_ref = refs
    rows = q_ref.shape[0]
    both = []
    for h, (peak, total, summed) in enumerate(attend(q_ref, kv_refs)):
        out_ref[:rows, h * HD : (h + 1) * HD] = (summed * (1.0 / total)).astype(BF)
        both.append(log_total(peak, total))
    rest = turned(*both)
    at = lax.broadcasted_iota(jnp.int32, (16, rows), 0)
    tail = jnp.zeros((16, rows), F32)
    for i in range(3):
        piece = rest.astype(BF).astype(F32)
        for h in range(2):
            tail = jnp.where(at == 3 * h + i, piece[h : h + 1], tail)
        rest = rest - piece
    out_ref[rows:, :] = tail.astype(BF)


def kept_body(q_ref, *refs):
    *kv_refs, o_ref, peak_ref, total_ref, out_ref, lse_ref = refs
    both = []
    starts = [
        (peak_ref[h][:, :1], total_ref[h][:, :1], o_ref[:, h * HD : (h + 1) * HD]) for h in range(2)
    ]
    for h in range(2):
        peak, total, summed = attend(q_ref, kv_refs, (h,), starts)[0]
        out_ref[:, h * HD : (h + 1) * HD] = summed * (1.0 / total)
        both.append(log_total(peak, total))
    lse_ref[...] = turned(*both)


def merge_body(own_ref, lse_ref, *refs):
    *got_refs, out_ref = refs
    rows = own_ref.shape[0]
    parts = len(got_refs) + 1
    at = lax.broadcasted_iota(jnp.int32, (HD, rows), 0)
    lanes = jnp.zeros((HD, rows), F32)
    tails = [got_ref[rows:, :].astype(F32) for got_ref in got_refs]
    for h in range(2):
        lse = [lse_ref[h : h + 1]] + [
            sum(tail[3 * h + i : 3 * h + i + 1] for i in range(3)) for tail in tails
        ]
        top = functools.reduce(jnp.maximum, lse)
        part = [jnp.exp(e - top) for e in lse]
        inverse = 1.0 / sum(part)
        for g, p in enumerate(part):
            lanes = jnp.where(at == parts * h + g, p * inverse, lanes)
    shares = jnp.transpose(lanes)
    for h in range(2):
        cols = slice(h * HD, (h + 1) * HD)
        merged = shares[:, parts * h : parts * h + 1] * own_ref[:, cols]
        for g, got_ref in enumerate(got_refs):
            share = shares[:, parts * h + g + 1 : parts * h + g + 2]
            merged = merged + share * got_ref[:rows, cols].astype(F32)
        out_ref[:, cols] = merged.astype(BF)


def out_body(mdl_ref, own_ref, other_ref, wa_ref, wb_ref, *refs):
    *out_refs, x = refs
    for s, chip in enumerate(slot_chips(mdl_ref[0], False)):
        for k in range(2):
            rows = pl.ds(pl.multiple_of(128 * k + 16 * chip, 16), 16)
            x[s * 32 + 16 * k : s * 32 + 16 * k + 16, :256] = own_ref[rows, :]
            x[s * 32 + 16 * k : s * 32 + 16 * k + 16, 256:] = other_ref[rows, :]
    for at in range(0, wa_ref.shape[1], 512):
        cols = slice(at, at + 512)
        r = jnp.dot(x[:, :256], wa_ref[:, cols], preferred_element_type=F32) + jnp.dot(
            x[:, 256:], wb_ref[:, cols], preferred_element_type=F32
        )
        for s, out_ref in enumerate(out_refs):
            out_ref[:, cols] = r[32 * s : 32 * s + 32].astype(BF)


def add_body(*refs):
    *in_refs, out_ref = refs
    out_ref[...] = sum(r[...].astype(F32) for r in in_refs).astype(BF)


def sum_body(core_ref, *refs):
    *in_refs, keep_ref, give_ref = refs
    k = core_ref[0]
    total = sum(r[...].astype(F32) for r in in_refs)
    keep_ref[...] = jnp.where(k == 0, total[:16], total[16:])
    give_ref[...] = jnp.where(k == 0, total[16:], total[:16])


def tail_body(
    core_ref, own_ref, other_ref, x_ref, gate_ref, scale_ref, wf_ref, state_ref, noise_ref,
    owner_ref, hidden_ref, next_ref, slot_ref, vel,
):
    k = core_ref[0]
    own, other = own_ref[...], other_ref[...]
    left = jnp.where(k == 0, own, other)
    right = jnp.where(k == 0, other, own)
    blocks, rows, width = x_ref.shape
    half = blocks // 2
    mixed = []
    square = jnp.zeros((rows, width), F32)
    for b in range(blocks):
        at = (b % half) * width
        part = (left if b < half else right)[:, at : at + width]
        mix = x_ref[b].astype(F32) + gate_ref[b : b + 1] * part
        hidden_ref[:, b * width : (b + 1) * width] = mix.astype(BF)
        square = square + mix * mix
        mixed.append(mix)
    inverse = lax.rsqrt(jnp.sum(square, -1, keepdims=True) / (blocks * width) + 1e-06)
    normed = jnp.concatenate(
        [
            (mixed[b] * inverse * (1.0 + scale_ref[b : b + 1])).astype(BF)
            for b in range(blocks)
        ],
        -1,
    )
    acc = lax.dot_general(
        normed, wf_ref[...], (((1,), (1,)), ((), ())), preferred_element_type=F32
    )
    vel[...] = acc
    tiles = state_ref.shape[0]
    lat = acc.shape[1]
    velocity = jnp.concatenate(
        [vel[pl.ds(j, tiles, stride=rows // tiles), :] for j in range(rows // tiles)], -1
    )
    state = state_ref[...]
    new = (
        state
        + 0.2 * (velocity + 0.5 * (0.5 * velocity - state) / (1.0 - 0.5))
        + math.sqrt(0.2) * noise_ref[...]
    )
    next_ref[...] = new
    panels = new.astype(BF).astype(F32)
    owned = slot_ref.shape[0] * CAP
    at = lax.broadcasted_iota(jnp.int32, (owned, panels.shape[1]), 0)
    slots = jnp.zeros(at.shape, F32)
    for t in range(tiles):
        owner = owner_ref[t]
        before = jnp.int32(0)
        for e in range(t):
            before = before + jnp.where(owner_ref[e] == owner, 1, 0)
        slots = jnp.where(at == owner * CAP + before, panels[t : t + 1], slots)
    for o in range(slot_ref.shape[0]):
        slot_ref[o] = slots[CAP * o : CAP * o + CAP]


def up_body(x_ref, w_ref, out_ref):
    x = jnp.concatenate([x_ref[o] for o in range(x_ref.shape[0])], 0).astype(BF)
    y = jnp.dot(x, w_ref[...], preferred_element_type=F32)
    out_ref[...] = jax.nn.gelu(y).astype(BF)


def shards(
    latents, mod_shift, mod_scale, gate, w_query, w_key, w_value, w_out, cache_keys,
    cache_values, final_scale, w_final, state, noise, owners, w_up,
):
    count, part = latents.shape
    mdl = lax.axis_index("mdl")
    core = mdl % 2
    core_1 = jnp.reshape(core, (1,)).astype(jnp.int32)
    mdl_1 = jnp.reshape(mdl, (1,)).astype(jnp.int32)
    chips = 8
    block = count // 16
    rows = count // 2

    cached = call(
        join_body,
        shape((cache_keys.shape[0], 2 * cache_keys.shape[1]), BF),
        (cache_keys, cache_values),
        hbm=(0, 1),
        scratch=[pltpu.SemaphoreType.DMA((2,))],
    )
    keep, give = call(
        turn_body,
        (shape((rows, part), BF), shape((rows, part), BF)),
        (core_1, latents.T),
        smem=(0,),
    )
    got = core_swap(give)
    is_first = core == 0
    wide = jnp.concatenate(
        [jnp.where(is_first, keep, got), jnp.where(is_first, got, keep)], 1
    )
    beside = pair_swap(wide)
    mine = [z_send(wide, by) for by in STEPS]
    x = [wide, beside] + mine + [z_send(beside, by) for by in STEPS]

    cached_in = y_swap(call(copy_body, shape(cached.shape, BF), (cached,), after=(beside,)))

    half = w_out.shape[1] // 2
    w_mine, w_give = call(
        halves_body,
        (shape((w_out.shape[0], half), BF), shape((w_out.shape[0], half), BF)),
        (core_1, w_out),
        smem=(0,),
        after=(x[5],),
    )
    w_theirs = core_swap(w_give)

    weights = call(
        load_body,
        tuple(shape(w.shape, BF) for w in (w_query, w_key, w_value)),
        (w_query, w_key, w_value),
        hbm=(0, 1, 2),
        nbytes=8 * MIB,
        scratch=[pltpu.SemaphoreType.DMA((3, 4))],
        limit=45,
        flops=5000000000,
        after=tuple(mine),
    )
    normed, own_x = call(
        norm_body,
        (shape((rows, chips * 2 * part), BF), shape((chips, block, 2 * part), BF)),
        (
            mdl_1, *x, mod_scale.reshape(chips, 2 * part), mod_shift.reshape(chips, 2 * part),
        ),
        smem=(0,),
        flops=MIB,
        nbytes=MIB,
        after=(w_mine, *weights),
    )
    cols = w_query.shape[1]
    normed_in = core_swap(normed)
    kv_half, query_half = call(
        half_body,
        (shape((rows, 2 * cols), BF), shape((rows, cols), BF)),
        (normed, weights[1], weights[2], weights[0]),
        after=(cached_in,),
        flops=30000000000,
        nbytes=8 * MIB,
    )
    kv_rest = call(
        kv_body,
        shape((rows, 2 * cols), BF),
        (normed_in, weights[1], weights[2]),
        flops=1 << 34,
        nbytes=5 * MIB,
    )
    query = call(
        query_body,
        shape((count, cols), BF),
        (core_1, normed_in, weights[0], query_half),
        smem=(0,),
        flops=2 * rows * w_query.shape[0] * cols,
        nbytes=3 * MIB,
    )
    fresh = [kv_half, kv_rest, y_swap(kv_half), y_swap(kv_rest)]
    query_in = [x_send(query, by) for by in STEPS]

    stats = call(
        past_body,
        (
            shape((count, cols), F32),
            shape((2, count, HD), F32),
            shape((2, count, HD), F32),
        ),
        (query, cached, cached_in),
        flops=MIB,
        nbytes=MIB,
    )
    back, before = [], stats[0]
    for by, q in zip(STEPS, query_in):
        before = call(
            sent_body,
            shape((count + 16, cols), BF),
            (q, cached, cached_in, *fresh),
            flops=MIB,
            nbytes=MIB,
            after=(before,),
        )
        back.append(x_send(before, -by))
    kept = call(
        kept_body,
        (shape((count, cols), F32), shape((8, count), F32)),
        (query, *fresh, *stats),
        flops=MIB,
        nbytes=MIB,
        after=(before,),
    )
    attended = call(merge_body, shape((count, cols), BF), (*kept, *back), nbytes=MIB)

    projected = call(
        out_body,
        tuple(shape((2 * block, half), BF) for _ in range(chips)),
        (mdl_1, attended, core_swap(attended), w_mine, w_theirs),
        smem=(0,),
        flops=2 * count * 512 * half,
        nbytes=4 * MIB,
        scratch=[pltpu.VMEM((count, 2 * cols), BF)],
    )
    def added(*parts, flops=0):
        return call(add_body, shape(parts[0].shape, BF), parts, flops=flops)

    across = pair_swap(projected[7])
    relayed = [z_send(projected[5], 1), z_send(projected[6], 3)]
    direct = [z_send(projected[2], 1), z_send(projected[3], 3)]
    direct.append(z_send(added(projected[4], across, flops=1 << 35), 2))
    passed = pair_swap(added(projected[1], *relayed))
    ours, theirs = call(
        sum_body,
        (shape((block, half), F32), shape((block, half), F32)),
        (core_1, projected[0], *direct, passed),
        smem=(0,),
        nbytes=2 * MIB,
    )
    hidden_out, next_state, slot_rows = call(
        tail_body,
        (
            shape((block, w_out.shape[1]), BF),
            shape(state.shape, F32),
            shape((16, CAP, state.shape[1]), F32),
        ),
        (
            core_1, ours, core_swap(theirs), own_x, gate.reshape(chips, 2 * part),
            final_scale.reshape(chips, 2 * part), w_final.T, state, noise, owners[:, 0],
        ),
        smem=(0, 9),
        nbytes=2 * MIB,
        scratch=[pltpu.VMEM((block, w_final.shape[1]), F32)],
    )
    routed = lax.all_to_all(slot_rows, "mdl", split_axis=0, concat_axis=0, tiled=True)
    upsampled = call(
        up_body, shape((16 * CAP, w_up.shape[1]), BF), (routed, w_up), nbytes=MIB
    )
    return (hidden_out, next_state, upsampled)


def solution(mesh):
    return jax.shard_map(
        shards,
        mesh=mesh,
        in_specs=(
            P("ctx", "mdl"),
            P(),
            P(),
            P(),
            P(None, "mdl"),
            P(None, "mdl"),
            P(None, "mdl"),
            P("mdl", None),
            P("ctx", "mdl"),
            P("ctx", "mdl"),
            P(),
            P(),
            P(("ctx", "mdl"), None),
            P(("ctx", "mdl"), None),
            P(("ctx", "mdl"), None),
            P(),
        ),
        out_specs=(P(("ctx", "mdl"), None), P(("ctx", "mdl"), None), P(("ctx", "mdl"), None)),
        check_vma=False,
    )
```

```python
import functools
import math

import jax
import jax.numpy as jnp
from jax import lax
from jax.experimental import pallas as pl
from jax.experimental.pallas import tpu as pltpu
from jax.sharding import PartitionSpec as P

HD = 128
CAP = 2
BF = jnp.bfloat16
F32 = jnp.float32
MIB = 1 << 20
VM = pl.BlockSpec(memory_space=pltpu.VMEM)
SM = pl.BlockSpec(memory_space=pltpu.SMEM)
HB = pl.BlockSpec(memory_space=pltpu.HBM)

CORE_SWAP = [(m, m ^ 1) for m in range(16)]
PAIR_SWAP = [(m, m ^ 2) for m in range(16)]
STEPS = (1, 3, 2)


def y_swap(a):
    return lax.ppermute(a, "ctx", [(c, c ^ 4) for c in range(8)])


def x_send(a, by):
    return lax.ppermute(a, "ctx", [(c, (c // 4) * 4 + (c + by) % 4) for c in range(8)])


def core_swap(a):
    return lax.ppermute(a, "mdl", CORE_SWAP)


def pair_swap(a):
    return lax.ppermute(a, "mdl", PAIR_SWAP)


def z_send(a, by):
    return lax.ppermute(a, "mdl", [(m, (m + 4 * by) % 16) for m in range(16)])


def slot_chips(mdl, back):
    z, h = mdl >> 2, (mdl >> 1) & 1
    around = [(z + (-by if back else by)) & 3 for by in STEPS]
    return [z * 2 + h, z * 2 + 1 - h] + [a * 2 + h for a in around] + [a * 2 + 1 - h for a in around]


def call(
    body, outs, args, flops=0, nbytes=0, trans=0, smem=(), hbm=(), scratch=(), limit=24, after=()
):
    count = len(args)
    place = [SM if i in smem else HB if i in hbm else VM for i in range(count)]

    def run(*refs):
        body(*refs[:count], *refs[count + len(after) :])

    return pl.pallas_call(
        run,
        out_shape=outs,
        in_specs=place
        + [pl.BlockSpec(memory_space=pl.ANY)] * len(after),
        out_specs=jax.tree.map(lambda o: VM, outs),
        scratch_shapes=list(scratch),
        compiler_params=pltpu.CompilerParams(vmem_limit_bytes=limit * MIB),
        cost_estimate=pl.CostEstimate(flops=flops, bytes_accessed=nbytes, transcendentals=trans),
    )(*args, *after)


def shape(dims, dtype):
    return jax.ShapeDtypeStruct(dims, dtype)


def turn_body(core_ref, x_ref, keep_ref, give_ref):
    k = core_ref[0]
    block = 16
    x = jnp.transpose(x_ref[...])
    for j in range(x.shape[0] // (2 * block)):
        first = x[2 * j * block : (2 * j + 1) * block]
        second = x[(2 * j + 1) * block : (2 * j + 2) * block]
        keep_ref[j * block : (j + 1) * block] = jnp.where(k == 0, first, second)
        give_ref[j * block : (j + 1) * block] = jnp.where(k == 0, second, first)


def copy_body(x_ref, out_ref):
    out_ref[...] = x_ref[...]


def join_body(a_ref, b_ref, out_ref, sems):
    width = a_ref.shape[1]
    copies = [
        pltpu.make_async_copy(ref, out_ref.at[:, pl.ds(i * width, width)], sems.at[i])
        for i, ref in enumerate((a_ref, b_ref))
    ]
    for copy in copies:
        copy.start()
    for copy in copies:
        copy.wait()


def load_body(*refs):
    *refs, sems = refs
    half = len(refs) // 2
    pieces = sems.shape[1]
    copies = []
    for i, (src, dst) in enumerate(zip(refs[:half], refs[half:])):
        some = src.shape[0] // pieces
        for j in range(pieces):
            rows = pl.ds(j * some, some)
            copies.append(pltpu.make_async_copy(src.at[rows], dst.at[rows], sems.at[i, j]))
    for copy in copies:
        copy.start()
    for copy in copies:
        copy.wait()


def halves_body(core_ref, w_ref, mine_ref, theirs_ref):
    k = core_ref[0]
    width = mine_ref.shape[1]
    mine_ref[...] = w_ref[:, pl.ds(pl.multiple_of(k * width, width), width)]
    theirs_ref[...] = w_ref[:, pl.ds(pl.multiple_of((1 - k) * width, width), width)]


def norm_body(mdl_ref, *refs):
    *x_refs, scale_ref, shift_ref, out_ref, own_ref = refs
    blocks = len(x_refs)
    rows, width = x_refs[0].shape
    total = sum(x_ref[...].astype(F32) for x_ref in x_refs)
    mean = jnp.sum(total, -1, keepdims=True) / (blocks * width)
    square = jnp.zeros((rows, width), F32)
    for x_ref in x_refs:
        centred = x_ref[...].astype(F32) - mean
        square = square + centred * centred
    var = jnp.sum(square, -1, keepdims=True) / (blocks * width)
    inverse = lax.rsqrt(var + 1e-06)
    chips = slot_chips(mdl_ref[0], True)
    block = own_ref.shape[1]
    here = pl.ds(pl.multiple_of(chips[0] * block, block), block)
    for chip, x_ref in zip(chips, x_refs):
        own_ref[chip] = x_ref[here, :]
        centred = x_ref[...].astype(F32) - mean
        scale, shift = scale_ref[pl.ds(chip, 1)], shift_ref[pl.ds(chip, 1)]
        cols = pl.ds(pl.multiple_of(chip * width, width), width)
        out_ref[:, cols] = (centred * inverse * (1.0 + scale) + shift).astype(BF)


def half_body(x_ref, wk_ref, wv_ref, wq_ref, kv_ref, q_ref):
    kv_ref[:, :256] = jnp.dot(x_ref[...], wk_ref[...], preferred_element_type=F32).astype(BF)
    kv_ref[:, 256:] = jnp.dot(x_ref[...], wv_ref[...], preferred_element_type=F32).astype(BF)
    q_ref[...] = jnp.dot(x_ref[...], wq_ref[...], preferred_element_type=F32).astype(BF)


def kv_body(x_ref, wk_ref, wv_ref, kv_ref):
    kv_ref[:, :256] = jnp.dot(x_ref[...], wk_ref[...], preferred_element_type=F32).astype(BF)
    kv_ref[:, 256:] = jnp.dot(x_ref[...], wv_ref[...], preferred_element_type=F32).astype(BF)


def query_body(core_ref, x_ref, wq_ref, half_ref, q_ref):
    k = core_ref[0]
    rows = x_ref.shape[0]
    q_ref[pl.ds(pl.multiple_of(k * rows, rows), rows), :] = half_ref[...]
    q_ref[pl.ds(pl.multiple_of((1 - k) * rows, rows), rows), :] = jnp.dot(
        x_ref[...], wq_ref[...], preferred_element_type=F32
    ).astype(BF)


C2 = math.log2(math.e) / math.sqrt(HD)


def fold(op, parts):
    return functools.reduce(
        op, [p[:, at : at + HD] for p in parts for at in range(0, p.shape[1], HD)]
    )


def attend(q_ref, kv_refs, which=(0, 1), starts=None):
    heads = [slice(h * HD, (h + 1) * HD) for h in which]
    every = [
        [
            lax.dot_general(
                q_ref[:, cols], kv[:, cols], (((1,), (1,)), ((), ())), preferred_element_type=F32
            )
            for kv in kv_refs
        ]
        for cols in heads
    ]
    results = []
    for h, scores in zip(which, every):
        peak = jnp.max(fold(jnp.maximum, scores), -1, keepdims=True)
        if starts is not None:
            peak = jnp.maximum(peak, starts[h][0])
        probs = [jnp.exp2((s - peak) * C2) for s in scores]
        total = jnp.sum(fold(jnp.add, probs), -1, keepdims=True)
        summed = sum(
            jnp.dot(
                p.astype(BF),
                kv[:, 256 + h * HD : 256 + (h + 1) * HD],
                preferred_element_type=F32,
            )
            for p, kv in zip(probs, kv_refs)
        )
        if starts is not None:
            factor = jnp.exp2((starts[h][0] - peak) * C2)
            total, summed = starts[h][1] * factor + total, starts[h][2] * factor + summed
        results.append((peak, total, summed))
    return results


def past_body(q_ref, *refs):
    *kv_refs, o_ref, peak_ref, total_ref = refs
    for h, (peak, total, summed) in enumerate(attend(q_ref, kv_refs)):
        o_ref[:, h * HD : (h + 1) * HD] = summed
        peak_ref[h] = jnp.broadcast_to(peak, peak_ref.shape[1:])
        total_ref[h] = jnp.broadcast_to(total, total_ref.shape[1:])


def log_total(peak, total):
    return peak / math.sqrt(HD) + jnp.log(total)


def turned(first, second):
    lane = lax.broadcasted_iota(jnp.int32, (first.shape[0], HD), 1)
    return jnp.transpose(jnp.where(lane == 0, first, second))[:8]


def sent_body(q_ref, *refs):
    *kv_refs, out_ref = refs
    rows = q_ref.shape[0]
    both = []
    for h, (peak, total, summed) in enumerate(attend(q_ref, kv_refs)):
        out_ref[:rows, h * HD : (h + 1) * HD] = (summed * (1.0 / total)).astype(BF)
        both.append(log_total(peak, total))
    rest = turned(*both)
    at = lax.broadcasted_iota(jnp.int32, (16, rows), 0)
    tail = jnp.zeros((16, rows), F32)
    for i in range(3):
        piece = rest.astype(BF).astype(F32)
        for h in range(2):
            tail = jnp.where(at == 3 * h + i, piece[h : h + 1], tail)
        rest = rest - piece
    out_ref[rows:, :] = tail.astype(BF)


def kept_body(q_ref, *refs):
    *kv_refs, o_ref, peak_ref, total_ref, out_ref, lse_ref = refs
    both = []
    starts = [
        (peak_ref[h][:, :1], total_ref[h][:, :1], o_ref[:, h * HD : (h + 1) * HD]) for h in range(2)
    ]
    for h in range(2):
        peak, total, summed = attend(q_ref, kv_refs, (h,), starts)[0]
        out_ref[:, h * HD : (h + 1) * HD] = summed * (1.0 / total)
        both.append(log_total(peak, total))
    lse_ref[...] = turned(*both)


def merge_body(own_ref, lse_ref, *refs):
    *got_refs, out_ref = refs
    rows = own_ref.shape[0]
    parts = len(got_refs) + 1
    at = lax.broadcasted_iota(jnp.int32, (HD, rows), 0)
    lanes = jnp.zeros((HD, rows), F32)
    tails = [got_ref[rows:, :].astype(F32) for got_ref in got_refs]
    for h in range(2):
        lse = [lse_ref[h : h + 1]] + [
            sum(tail[3 * h + i : 3 * h + i + 1] for i in range(3)) for tail in tails
        ]
        top = functools.reduce(jnp.maximum, lse)
        part = [jnp.exp(e - top) for e in lse]
        inverse = 1.0 / sum(part)
        for g, p in enumerate(part):
            lanes = jnp.where(at == parts * h + g, p * inverse, lanes)
    shares = jnp.transpose(lanes)
    for h in range(2):
        cols = slice(h * HD, (h + 1) * HD)
        merged = shares[:, parts * h : parts * h + 1] * own_ref[:, cols]
        for g, got_ref in enumerate(got_refs):
            share = shares[:, parts * h + g + 1 : parts * h + g + 2]
            merged = merged + share * got_ref[:rows, cols].astype(F32)
        out_ref[:, cols] = merged.astype(BF)


def out_body(mdl_ref, own_ref, other_ref, wa_ref, wb_ref, *refs):
    *out_refs, x = refs
    for s, chip in enumerate(slot_chips(mdl_ref[0], False)):
        for k in range(2):
            rows = pl.ds(pl.multiple_of(128 * k + 16 * chip, 16), 16)
            x[s * 32 + 16 * k : s * 32 + 16 * k + 16, :256] = own_ref[rows, :]
            x[s * 32 + 16 * k : s * 32 + 16 * k + 16, 256:] = other_ref[rows, :]
    for at in range(0, wa_ref.shape[1], 512):
        cols = slice(at, at + 512)
        r = jnp.dot(x[:, :256], wa_ref[:, cols], preferred_element_type=F32) + jnp.dot(
            x[:, 256:], wb_ref[:, cols], preferred_element_type=F32
        )
        for s, out_ref in enumerate(out_refs):
            out_ref[:, cols] = r[32 * s : 32 * s + 32].astype(BF)


def add_body(*refs):
    *in_refs, out_ref = refs
    out_ref[...] = sum(r[...].astype(F32) for r in in_refs).astype(BF)


def sum_body(core_ref, *refs):
    *in_refs, keep_ref, give_ref = refs
    k = core_ref[0]
    total = sum(r[...].astype(F32) for r in in_refs)
    keep_ref[...] = jnp.where(k == 0, total[:16], total[16:])
    give_ref[...] = jnp.where(k == 0, total[16:], total[:16])


def tail_body(
    core_ref, own_ref, other_ref, x_ref, gate_ref, scale_ref, wf_ref, state_ref, noise_ref,
    owner_ref, hidden_ref, next_ref, slot_ref, vel,
):
    k = core_ref[0]
    own, other = own_ref[...], other_ref[...]
    left = jnp.where(k == 0, own, other)
    right = jnp.where(k == 0, other, own)
    blocks, rows, width = x_ref.shape
    half = blocks // 2
    mixed = []
    square = jnp.zeros((rows, width), F32)
    for b in range(blocks):
        at = (b % half) * width
        part = (left if b < half else right)[:, at : at + width]
        mix = x_ref[b].astype(F32) + gate_ref[b : b + 1] * part
        hidden_ref[:, b * width : (b + 1) * width] = mix.astype(BF)
        square = square + mix * mix
        mixed.append(mix)
    inverse = lax.rsqrt(jnp.sum(square, -1, keepdims=True) / (blocks * width) + 1e-06)
    normed = jnp.concatenate(
        [
            (mixed[b] * inverse * (1.0 + scale_ref[b : b + 1])).astype(BF)
            for b in range(blocks)
        ],
        -1,
    )
    acc = lax.dot_general(
        normed, wf_ref[...], (((1,), (1,)), ((), ())), preferred_element_type=F32
    )
    vel[...] = acc
    tiles = state_ref.shape[0]
    lat = acc.shape[1]
    velocity = jnp.concatenate(
        [vel[pl.ds(j, tiles, stride=rows // tiles), :] for j in range(rows // tiles)], -1
    )
    state = state_ref[...]
    new = (
        state
        + 0.2 * (velocity + 0.5 * (0.5 * velocity - state) / (1.0 - 0.5))
        + math.sqrt(0.2) * noise_ref[...]
    )
    next_ref[...] = new
    panels = new.astype(BF).astype(F32)
    owned = slot_ref.shape[0] * CAP
    at = lax.broadcasted_iota(jnp.int32, (owned, panels.shape[1]), 0)
    slots = jnp.zeros(at.shape, F32)
    for t in range(tiles):
        owner = owner_ref[t]
        before = jnp.int32(0)
        for e in range(t):
            before = before + jnp.where(owner_ref[e] == owner, 1, 0)
        slots = jnp.where(at == owner * CAP + before, panels[t : t + 1], slots)
    for o in range(slot_ref.shape[0]):
        slot_ref[o] = slots[CAP * o : CAP * o + CAP]


def up_body(x_ref, w_ref, out_ref):
    x = jnp.concatenate([x_ref[o] for o in range(x_ref.shape[0])], 0).astype(BF)
    y = jnp.dot(x, w_ref[...], preferred_element_type=F32)
    out_ref[...] = jax.nn.gelu(y).astype(BF)


def shards(
    latents, mod_shift, mod_scale, gate, w_query, w_key, w_value, w_out, cache_keys,
    cache_values, final_scale, w_final, state, noise, owners, w_up,
):
    count, part = latents.shape
    mdl = lax.axis_index("mdl")
    core = mdl % 2
    core_1 = jnp.reshape(core, (1,)).astype(jnp.int32)
    mdl_1 = jnp.reshape(mdl, (1,)).astype(jnp.int32)
    chips = 8
    block = count // 16
    rows = count // 2

    cached = call(
        join_body,
        shape((cache_keys.shape[0], 2 * cache_keys.shape[1]), BF),
        (cache_keys, cache_values),
        hbm=(0, 1),
        scratch=[pltpu.SemaphoreType.DMA((2,))],
    )
    keep, give = call(
        turn_body,
        (shape((rows, part), BF), shape((rows, part), BF)),
        (core_1, latents.T),
        smem=(0,),
    )
    got = core_swap(give)
    is_first = core == 0
    wide = jnp.concatenate(
        [jnp.where(is_first, keep, got), jnp.where(is_first, got, keep)], 1
    )
    beside = pair_swap(wide)
    mine = [z_send(wide, by) for by in STEPS]
    x = [wide, beside] + mine + [z_send(beside, by) for by in STEPS]

    cached_in = y_swap(call(copy_body, shape(cached.shape, BF), (cached,), after=(beside,)))

    half = w_out.shape[1] // 2
    w_mine, w_give = call(
        halves_body,
        (shape((w_out.shape[0], half), BF), shape((w_out.shape[0], half), BF)),
        (core_1, w_out),
        smem=(0,),
        after=(x[5],),
    )
    w_theirs = core_swap(w_give)

    weights = call(
        load_body,
        tuple(shape(w.shape, BF) for w in (w_query, w_key, w_value)),
        (w_query, w_key, w_value),
        hbm=(0, 1, 2),
        nbytes=8 * MIB,
        scratch=[pltpu.SemaphoreType.DMA((3, 4))],
        limit=45,
        flops=5000000000,
        after=tuple(mine),
    )
    normed, own_x = call(
        norm_body,
        (shape((rows, chips * 2 * part), BF), shape((chips, block, 2 * part), BF)),
        (
            mdl_1, *x, mod_scale.reshape(chips, 2 * part), mod_shift.reshape(chips, 2 * part),
        ),
        smem=(0,),
        flops=MIB,
        nbytes=MIB,
        after=(w_mine, *weights),
    )
    cols = w_query.shape[1]
    normed_in = core_swap(normed)
    kv_half, query_half = call(
        half_body,
        (shape((rows, 2 * cols), BF), shape((rows, cols), BF)),
        (normed, weights[1], weights[2], weights[0]),
        after=(cached_in,),
        flops=30000000000,
        nbytes=8 * MIB,
    )
    kv_rest = call(
        kv_body,
        shape((rows, 2 * cols), BF),
        (normed_in, weights[1], weights[2]),
        flops=1 << 34,
        nbytes=5 * MIB,
    )
    query = call(
        query_body,
        shape((count, cols), BF),
        (core_1, normed_in, weights[0], query_half),
        smem=(0,),
        flops=2 * rows * w_query.shape[0] * cols,
        nbytes=3 * MIB,
    )
    fresh = [kv_half, kv_rest, y_swap(kv_half), y_swap(kv_rest)]
    query_in = [x_send(query, by) for by in STEPS]

    stats = call(
        past_body,
        (
            shape((count, cols), F32),
            shape((2, count, HD), F32),
            shape((2, count, HD), F32),
        ),
        (query, cached, cached_in),
        flops=MIB,
        nbytes=MIB,
    )
    back, before = [], stats[0]
    for by, q in zip(STEPS, query_in):
        before = call(
            sent_body,
            shape((count + 16, cols), BF),
            (q, cached, cached_in, *fresh),
            flops=MIB,
            nbytes=MIB,
            after=(before,),
        )
        back.append(x_send(before, -by))
    kept = call(
        kept_body,
        (shape((count, cols), F32), shape((8, count), F32)),
        (query, *fresh, *stats),
        flops=MIB,
        nbytes=MIB,
        after=(before,),
    )
    for i in range(2):
        back[i] = call(
            copy_body, shape(back[i].shape, BF), (back[i],), flops=1 << 28, after=tuple(back[:i])
        )
    attended = call(merge_body, shape((count, cols), BF), (*kept, *back), nbytes=MIB)

    projected = call(
        out_body,
        tuple(shape((2 * block, half), BF) for _ in range(chips)),
        (mdl_1, attended, core_swap(attended), w_mine, w_theirs),
        smem=(0,),
        flops=2 * count * 512 * half,
        nbytes=4 * MIB,
        scratch=[pltpu.VMEM((count, 2 * cols), BF)],
    )
    def added(*parts, flops=0):
        return call(add_body, shape(parts[0].shape, BF), parts, flops=flops)

    across = pair_swap(projected[7])
    relayed = [z_send(projected[5], 1), z_send(projected[6], 3)]
    direct = [z_send(projected[2], 1), z_send(projected[3], 3)]
    direct.append(z_send(added(projected[4], across, flops=1 << 35), 2))
    passed = pair_swap(added(projected[1], *relayed))
    ours, theirs = call(
        sum_body,
        (shape((block, half), F32), shape((block, half), F32)),
        (core_1, projected[0], *direct, passed),
        smem=(0,),
        nbytes=2 * MIB,
    )
    hidden_out, next_state, slot_rows = call(
        tail_body,
        (
            shape((block, w_out.shape[1]), BF),
            shape(state.shape, F32),
            shape((16, CAP, state.shape[1]), F32),
        ),
        (
            core_1, ours, core_swap(theirs), own_x, gate.reshape(chips, 2 * part),
            final_scale.reshape(chips, 2 * part), w_final.T, state, noise, owners[:, 0],
        ),
        smem=(0, 9),
        nbytes=2 * MIB,
        scratch=[pltpu.VMEM((block, w_final.shape[1]), F32)],
    )
    routed = lax.all_to_all(slot_rows, "mdl", split_axis=0, concat_axis=0, tiled=True)
    upsampled = call(
        up_body, shape((16 * CAP, w_up.shape[1]), BF), (routed, w_up), nbytes=MIB
    )
    return (hidden_out, next_state, upsampled)


def solution(mesh):
    return jax.shard_map(
        shards,
        mesh=mesh,
        in_specs=(
            P("ctx", "mdl"),
            P(),
            P(),
            P(),
            P(None, "mdl"),
            P(None, "mdl"),
            P(None, "mdl"),
            P("mdl", None),
            P("ctx", "mdl"),
            P("ctx", "mdl"),
            P(),
            P(),
            P(("ctx", "mdl"), None),
            P(("ctx", "mdl"), None),
            P(("ctx", "mdl"), None),
            P(),
        ),
        out_specs=(P(("ctx", "mdl"), None), P(("ctx", "mdl"), None), P(("ctx", "mdl"), None)),
        check_vma=False,
    )
```

```python
import functools
import math

import jax
import jax.numpy as jnp
from jax import lax
from jax.experimental import pallas as pl
from jax.experimental.pallas import tpu as pltpu
from jax.sharding import PartitionSpec as P

HD = 128
CAP = 2
BF = jnp.bfloat16
F32 = jnp.float32
MIB = 1 << 20
VM = pl.BlockSpec(memory_space=pltpu.VMEM)
SM = pl.BlockSpec(memory_space=pltpu.SMEM)
HB = pl.BlockSpec(memory_space=pltpu.HBM)

CORE_SWAP = [(m, m ^ 1) for m in range(16)]
PAIR_SWAP = [(m, m ^ 2) for m in range(16)]
STEPS = (1, 3, 2)


def y_swap(a):
    return lax.ppermute(a, "ctx", [(c, c ^ 4) for c in range(8)])


def x_send(a, by):
    return lax.ppermute(a, "ctx", [(c, (c // 4) * 4 + (c + by) % 4) for c in range(8)])


def core_swap(a):
    return lax.ppermute(a, "mdl", CORE_SWAP)


def pair_swap(a):
    return lax.ppermute(a, "mdl", PAIR_SWAP)


def z_send(a, by):
    return lax.ppermute(a, "mdl", [(m, (m + 4 * by) % 16) for m in range(16)])


def slot_chips(mdl, back):
    z, h = mdl >> 2, (mdl >> 1) & 1
    around = [(z + (-by if back else by)) & 3 for by in STEPS]
    return [z * 2 + h, z * 2 + 1 - h] + [a * 2 + h for a in around] + [a * 2 + 1 - h for a in around]


def call(
    body, outs, args, flops=0, nbytes=0, trans=0, smem=(), hbm=(), scratch=(), limit=24, after=()
):
    count = len(args)
    place = [SM if i in smem else HB if i in hbm else VM for i in range(count)]

    def run(*refs):
        body(*refs[:count], *refs[count + len(after) :])

    return pl.pallas_call(
        run,
        out_shape=outs,
        in_specs=place
        + [pl.BlockSpec(memory_space=pl.ANY)] * len(after),
        out_specs=jax.tree.map(lambda o: VM, outs),
        scratch_shapes=list(scratch),
        compiler_params=pltpu.CompilerParams(vmem_limit_bytes=limit * MIB),
        cost_estimate=pl.CostEstimate(flops=flops, bytes_accessed=nbytes, transcendentals=trans),
    )(*args, *after)


def shape(dims, dtype):
    return jax.ShapeDtypeStruct(dims, dtype)


def turn_body(core_ref, x_ref, keep_ref, give_ref):
    k = core_ref[0]
    block = 16
    x = jnp.transpose(x_ref[...])
    for j in range(x.shape[0] // (2 * block)):
        first = x[2 * j * block : (2 * j + 1) * block]
        second = x[(2 * j + 1) * block : (2 * j + 2) * block]
        keep_ref[j * block : (j + 1) * block] = jnp.where(k == 0, first, second)
        give_ref[j * block : (j + 1) * block] = jnp.where(k == 0, second, first)


def copy_body(x_ref, out_ref):
    out_ref[...] = x_ref[...]


def join_body(a_ref, b_ref, out_ref, sems):
    width = a_ref.shape[1]
    copies = [
        pltpu.make_async_copy(ref, out_ref.at[:, pl.ds(i * width, width)], sems.at[i])
        for i, ref in enumerate((a_ref, b_ref))
    ]
    for copy in copies:
        copy.start()
    for copy in copies:
        copy.wait()


def load_body(*refs):
    *refs, sems = refs
    half = len(refs) // 2
    pieces = sems.shape[1]
    copies = []
    for i, (src, dst) in enumerate(zip(refs[:half], refs[half:])):
        some = src.shape[0] // pieces
        for j in range(pieces):
            rows = pl.ds(j * some, some)
            copies.append(pltpu.make_async_copy(src.at[rows], dst.at[rows], sems.at[i, j]))
    for copy in copies:
        copy.start()
    for copy in copies:
        copy.wait()


def halves_body(core_ref, w_ref, mine_ref, theirs_ref):
    k = core_ref[0]
    width = mine_ref.shape[1]
    mine_ref[...] = w_ref[:, pl.ds(pl.multiple_of(k * width, width), width)]
    theirs_ref[...] = w_ref[:, pl.ds(pl.multiple_of((1 - k) * width, width), width)]


def norm_body(mdl_ref, *refs):
    *x_refs, scale_ref, shift_ref, out_ref, own_ref = refs
    blocks = len(x_refs)
    rows, width = x_refs[0].shape
    total = sum(x_ref[...].astype(F32) for x_ref in x_refs)
    mean = jnp.sum(total, -1, keepdims=True) / (blocks * width)
    square = jnp.zeros((rows, width), F32)
    for x_ref in x_refs:
        centred = x_ref[...].astype(F32) - mean
        square = square + centred * centred
    var = jnp.sum(square, -1, keepdims=True) / (blocks * width)
    inverse = lax.rsqrt(var + 1e-06)
    chips = slot_chips(mdl_ref[0], True)
    block = own_ref.shape[1]
    here = pl.ds(pl.multiple_of(chips[0] * block, block), block)
    for chip, x_ref in zip(chips, x_refs):
        own_ref[chip] = x_ref[here, :]
        centred = x_ref[...].astype(F32) - mean
        scale, shift = scale_ref[pl.ds(chip, 1)], shift_ref[pl.ds(chip, 1)]
        cols = pl.ds(pl.multiple_of(chip * width, width), width)
        out_ref[:, cols] = (centred * inverse * (1.0 + scale) + shift).astype(BF)


def half_body(x_ref, wk_ref, wv_ref, wq_ref, kv_ref, q_ref):
    kv_ref[:, :256] = jnp.dot(x_ref[...], wk_ref[...], preferred_element_type=F32).astype(BF)
    kv_ref[:, 256:] = jnp.dot(x_ref[...], wv_ref[...], preferred_element_type=F32).astype(BF)
    q_ref[...] = jnp.dot(x_ref[...], wq_ref[...], preferred_element_type=F32).astype(BF)


def kv_body(x_ref, wk_ref, wv_ref, kv_ref):
    kv_ref[:, :256] = jnp.dot(x_ref[...], wk_ref[...], preferred_element_type=F32).astype(BF)
    kv_ref[:, 256:] = jnp.dot(x_ref[...], wv_ref[...], preferred_element_type=F32).astype(BF)


def query_body(core_ref, x_ref, wq_ref, half_ref, q_ref):
    k = core_ref[0]
    rows = x_ref.shape[0]
    q_ref[pl.ds(pl.multiple_of(k * rows, rows), rows), :] = half_ref[...]
    q_ref[pl.ds(pl.multiple_of((1 - k) * rows, rows), rows), :] = jnp.dot(
        x_ref[...], wq_ref[...], preferred_element_type=F32
    ).astype(BF)


C2 = math.log2(math.e) / math.sqrt(HD)


def fold(op, parts):
    return functools.reduce(
        op, [p[:, at : at + HD] for p in parts for at in range(0, p.shape[1], HD)]
    )


def attend(q_ref, kv_refs, which=(0, 1), starts=None):
    heads = [slice(h * HD, (h + 1) * HD) for h in which]
    every = [
        [
            lax.dot_general(
                q_ref[:, cols], kv[:, cols], (((1,), (1,)), ((), ())), preferred_element_type=F32
            )
            for kv in kv_refs
        ]
        for cols in heads
    ]
    results = []
    for h, scores in zip(which, every):
        peak = jnp.max(fold(jnp.maximum, scores), -1, keepdims=True)
        if starts is not None:
            peak = jnp.maximum(peak, starts[h][0])
        probs = [jnp.exp2((s - peak) * C2) for s in scores]
        total = jnp.sum(fold(jnp.add, probs), -1, keepdims=True)
        summed = sum(
            jnp.dot(
                p.astype(BF),
                kv[:, 256 + h * HD : 256 + (h + 1) * HD],
                preferred_element_type=F32,
            )
            for p, kv in zip(probs, kv_refs)
        )
        if starts is not None:
            factor = jnp.exp2((starts[h][0] - peak) * C2)
            total, summed = starts[h][1] * factor + total, starts[h][2] * factor + summed
        results.append((peak, total, summed))
    return results


def past_body(q_ref, *refs):
    *kv_refs, o_ref, peak_ref, total_ref = refs
    for h, (peak, total, summed) in enumerate(attend(q_ref, kv_refs)):
        o_ref[:, h * HD : (h + 1) * HD] = summed
        peak_ref[h] = jnp.broadcast_to(peak, peak_ref.shape[1:])
        total_ref[h] = jnp.broadcast_to(total, total_ref.shape[1:])


def log_total(peak, total):
    return peak / math.sqrt(HD) + jnp.log(total)


def turned(first, second):
    lane = lax.broadcasted_iota(jnp.int32, (first.shape[0], HD), 1)
    return jnp.transpose(jnp.where(lane == 0, first, second))[:8]


def sent_body(q_ref, *refs):
    *kv_refs, out_ref = refs
    rows = q_ref.shape[0]
    both = []
    for h, (peak, total, summed) in enumerate(attend(q_ref, kv_refs)):
        out_ref[:rows, h * HD : (h + 1) * HD] = (summed * (1.0 / total)).astype(BF)
        both.append(log_total(peak, total))
    rest = turned(*both)
    at = lax.broadcasted_iota(jnp.int32, (16, rows), 0)
    tail = jnp.zeros((16, rows), F32)
    for i in range(3):
        piece = rest.astype(BF).astype(F32)
        for h in range(2):
            tail = jnp.where(at == 3 * h + i, piece[h : h + 1], tail)
        rest = rest - piece
    out_ref[rows:, :] = tail.astype(BF)


def kept_body(q_ref, *refs):
    *kv_refs, o_ref, peak_ref, total_ref, out_ref, lse_ref = refs
    both = []
    starts = [
        (peak_ref[h][:, :1], total_ref[h][:, :1], o_ref[:, h * HD : (h + 1) * HD]) for h in range(2)
    ]
    for h in range(2):
        peak, total, summed = attend(q_ref, kv_refs, (h,), starts)[0]
        out_ref[:, h * HD : (h + 1) * HD] = summed * (1.0 / total)
        both.append(log_total(peak, total))
    lse_ref[...] = turned(*both)


def merge_body(own_ref, lse_ref, *refs):
    *got_refs, out_ref = refs
    rows = own_ref.shape[0]
    parts = len(got_refs) + 1
    at = lax.broadcasted_iota(jnp.int32, (HD, rows), 0)
    lanes = jnp.zeros((HD, rows), F32)
    tails = [got_ref[rows:, :].astype(F32) for got_ref in got_refs]
    for h in range(2):
        lse = [lse_ref[h : h + 1]] + [
            sum(tail[3 * h + i : 3 * h + i + 1] for i in range(3)) for tail in tails
        ]
        top = functools.reduce(jnp.maximum, lse)
        part = [jnp.exp(e - top) for e in lse]
        inverse = 1.0 / sum(part)
        for g, p in enumerate(part):
            lanes = jnp.where(at == parts * h + g, p * inverse, lanes)
    shares = jnp.transpose(lanes)
    for h in range(2):
        cols = slice(h * HD, (h + 1) * HD)
        merged = shares[:, parts * h : parts * h + 1] * own_ref[:, cols]
        for g, got_ref in enumerate(got_refs):
            share = shares[:, parts * h + g + 1 : parts * h + g + 2]
            merged = merged + share * got_ref[:rows, cols].astype(F32)
        out_ref[:, cols] = merged.astype(BF)


def in_slots(mdl_ref, own_ref, x):
    for s, chip in enumerate(slot_chips(mdl_ref[0], False)):
        for k in range(2):
            rows = pl.ds(pl.multiple_of(128 * k + 16 * chip, 16), 16)
            x[s * 32 + 16 * k : s * 32 + 16 * k + 16, :] = own_ref[rows, :]


def own_out_body(mdl_ref, own_ref, w_ref, part_ref, x):
    in_slots(mdl_ref, own_ref, x)
    for at in range(0, w_ref.shape[1], 512):
        cols = slice(at, at + 512)
        part_ref[:, cols] = jnp.dot(x[...], w_ref[:, cols], preferred_element_type=F32)


def out_body(mdl_ref, other_ref, w_ref, part_ref, *refs):
    *out_refs, x = refs
    in_slots(mdl_ref, other_ref, x)
    for at in range(0, w_ref.shape[1], 512):
        cols = slice(at, at + 512)
        r = part_ref[:, cols] + jnp.dot(x[...], w_ref[:, cols], preferred_element_type=F32)
        for s, out_ref in enumerate(out_refs):
            out_ref[:, cols] = r[32 * s : 32 * s + 32].astype(BF)


def add_body(*refs):
    *in_refs, out_ref = refs
    out_ref[...] = sum(r[...].astype(F32) for r in in_refs).astype(BF)


def sum_body(core_ref, *refs):
    *in_refs, keep_ref, give_ref = refs
    k = core_ref[0]
    total = sum(r[...].astype(F32) for r in in_refs)
    keep_ref[...] = jnp.where(k == 0, total[:16], total[16:])
    give_ref[...] = jnp.where(k == 0, total[16:], total[:16])


def tail_body(
    core_ref, own_ref, other_ref, x_ref, gate_ref, scale_ref, wf_ref, state_ref, noise_ref,
    owner_ref, hidden_ref, next_ref, slot_ref, vel,
):
    k = core_ref[0]
    own, other = own_ref[...], other_ref[...]
    left = jnp.where(k == 0, own, other)
    right = jnp.where(k == 0, other, own)
    blocks, rows, width = x_ref.shape
    half = blocks // 2
    mixed = []
    square = jnp.zeros((rows, width), F32)
    for b in range(blocks):
        at = (b % half) * width
        part = (left if b < half else right)[:, at : at + width]
        mix = x_ref[b].astype(F32) + gate_ref[b : b + 1] * part
        hidden_ref[:, b * width : (b + 1) * width] = mix.astype(BF)
        square = square + mix * mix
        mixed.append(mix)
    inverse = lax.rsqrt(jnp.sum(square, -1, keepdims=True) / (blocks * width) + 1e-06)
    normed = jnp.concatenate(
        [
            (mixed[b] * inverse * (1.0 + scale_ref[b : b + 1])).astype(BF)
            for b in range(blocks)
        ],
        -1,
    )
    acc = lax.dot_general(
        normed, wf_ref[...], (((1,), (1,)), ((), ())), preferred_element_type=F32
    )
    vel[...] = acc
    tiles = state_ref.shape[0]
    lat = acc.shape[1]
    velocity = jnp.concatenate(
        [vel[pl.ds(j, tiles, stride=rows // tiles), :] for j in range(rows // tiles)], -1
    )
    state = state_ref[...]
    new = (
        state
        + 0.2 * (velocity + 0.5 * (0.5 * velocity - state) / (1.0 - 0.5))
        + math.sqrt(0.2) * noise_ref[...]
    )
    next_ref[...] = new
    panels = new.astype(BF).astype(F32)
    owned = slot_ref.shape[0] * CAP
    at = lax.broadcasted_iota(jnp.int32, (owned, panels.shape[1]), 0)
    slots = jnp.zeros(at.shape, F32)
    for t in range(tiles):
        owner = owner_ref[t]
        before = jnp.int32(0)
        for e in range(t):
            before = before + jnp.where(owner_ref[e] == owner, 1, 0)
        slots = jnp.where(at == owner * CAP + before, panels[t : t + 1], slots)
    for o in range(slot_ref.shape[0]):
        slot_ref[o] = slots[CAP * o : CAP * o + CAP]


def up_body(x_ref, w_ref, out_ref):
    x = jnp.concatenate([x_ref[o] for o in range(x_ref.shape[0])], 0).astype(BF)
    y = jnp.dot(x, w_ref[...], preferred_element_type=F32)
    out_ref[...] = jax.nn.gelu(y).astype(BF)


def shards(
    latents, mod_shift, mod_scale, gate, w_query, w_key, w_value, w_out, cache_keys,
    cache_values, final_scale, w_final, state, noise, owners, w_up,
):
    count, part = latents.shape
    mdl = lax.axis_index("mdl")
    core = mdl % 2
    core_1 = jnp.reshape(core, (1,)).astype(jnp.int32)
    mdl_1 = jnp.reshape(mdl, (1,)).astype(jnp.int32)
    chips = 8
    block = count // 16
    rows = count // 2

    cached = call(
        join_body,
        shape((cache_keys.shape[0], 2 * cache_keys.shape[1]), BF),
        (cache_keys, cache_values),
        hbm=(0, 1),
        scratch=[pltpu.SemaphoreType.DMA((2,))],
    )
    keep, give = call(
        turn_body,
        (shape((rows, part), BF), shape((rows, part), BF)),
        (core_1, latents.T),
        smem=(0,),
    )
    got = core_swap(give)
    is_first = core == 0
    wide = jnp.concatenate(
        [jnp.where(is_first, keep, got), jnp.where(is_first, got, keep)], 1
    )
    beside = pair_swap(wide)
    mine = [z_send(wide, by) for by in STEPS]
    x = [wide, beside] + mine + [z_send(beside, by) for by in STEPS]

    cached_in = y_swap(call(copy_body, shape(cached.shape, BF), (cached,), after=(beside,)))

    half = w_out.shape[1] // 2
    w_mine, w_give = call(
        halves_body,
        (shape((w_out.shape[0], half), BF), shape((w_out.shape[0], half), BF)),
        (core_1, w_out),
        smem=(0,),
        after=(x[5],),
    )
    w_theirs = core_swap(w_give)

    weights = call(
        load_body,
        tuple(shape(w.shape, BF) for w in (w_query, w_key, w_value)),
        (w_query, w_key, w_value),
        hbm=(0, 1, 2),
        nbytes=8 * MIB,
        scratch=[pltpu.SemaphoreType.DMA((3, 4))],
        limit=45,
        flops=5000000000,
        after=tuple(mine),
    )
    normed, own_x = call(
        norm_body,
        (shape((rows, chips * 2 * part), BF), shape((chips, block, 2 * part), BF)),
        (
            mdl_1, *x, mod_scale.reshape(chips, 2 * part), mod_shift.reshape(chips, 2 * part),
        ),
        smem=(0,),
        flops=MIB,
        nbytes=MIB,
        after=(w_mine, *weights),
    )
    cols = w_query.shape[1]
    normed_in = core_swap(normed)
    kv_half, query_half = call(
        half_body,
        (shape((rows, 2 * cols), BF), shape((rows, cols), BF)),
        (normed, weights[1], weights[2], weights[0]),
        after=(cached_in,),
        flops=30000000000,
        nbytes=8 * MIB,
    )
    kv_rest = call(
        kv_body,
        shape((rows, 2 * cols), BF),
        (normed_in, weights[1], weights[2]),
        flops=1 << 34,
        nbytes=5 * MIB,
    )
    query = call(
        query_body,
        shape((count, cols), BF),
        (core_1, normed_in, weights[0], query_half),
        smem=(0,),
        flops=2 * rows * w_query.shape[0] * cols,
        nbytes=3 * MIB,
    )
    fresh = [kv_half, kv_rest, y_swap(kv_half), y_swap(kv_rest)]
    query_in = [x_send(query, by) for by in STEPS]

    stats = call(
        past_body,
        (
            shape((count, cols), F32),
            shape((2, count, HD), F32),
            shape((2, count, HD), F32),
        ),
        (query, cached, cached_in),
        flops=MIB,
        nbytes=MIB,
    )
    back, before = [], stats[0]
    for by, q in zip(STEPS, query_in):
        before = call(
            sent_body,
            shape((count + 16, cols), BF),
            (q, cached, cached_in, *fresh),
            flops=MIB,
            nbytes=MIB,
            after=(before,),
        )
        back.append(x_send(before, -by))
    kept = call(
        kept_body,
        (shape((count, cols), F32), shape((8, count), F32)),
        (query, *fresh, *stats),
        flops=MIB,
        nbytes=MIB,
        after=(before,),
    )
    for i in range(2):
        back[i] = call(
            copy_body, shape(back[i].shape, BF), (back[i],), flops=1 << 28, after=tuple(back[:i])
        )
    attended = call(merge_body, shape((count, cols), BF), (*kept, *back), nbytes=MIB)

    part_out = call(
        own_out_body,
        shape((count, half), F32),
        (mdl_1, attended, w_mine),
        smem=(0,),
        flops=2 * count * 256 * half,
        nbytes=4 * MIB,
        scratch=[pltpu.VMEM((count, cols), BF)],
    )
    projected = call(
        out_body,
        tuple(shape((2 * block, half), BF) for _ in range(chips)),
        (mdl_1, core_swap(attended), w_theirs, part_out),
        smem=(0,),
        flops=2 * count * 512 * half,
        nbytes=4 * MIB,
        scratch=[pltpu.VMEM((count, cols), BF)],
    )
    def added(*parts, flops=0):
        return call(add_body, shape(parts[0].shape, BF), parts, flops=flops)

    across = pair_swap(projected[7])
    relayed = [z_send(projected[5], 1), z_send(projected[6], 3)]
    direct = [z_send(projected[2], 1), z_send(projected[3], 3)]
    direct.append(z_send(added(projected[4], across, flops=1 << 35), 2))
    passed = pair_swap(added(projected[1], *relayed))
    ours, theirs = call(
        sum_body,
        (shape((block, half), F32), shape((block, half), F32)),
        (core_1, projected[0], *direct, passed),
        smem=(0,),
        nbytes=2 * MIB,
    )
    hidden_out, next_state, slot_rows = call(
        tail_body,
        (
            shape((block, w_out.shape[1]), BF),
            shape(state.shape, F32),
            shape((16, CAP, state.shape[1]), F32),
        ),
        (
            core_1, ours, core_swap(theirs), own_x, gate.reshape(chips, 2 * part),
            final_scale.reshape(chips, 2 * part), w_final.T, state, noise, owners[:, 0],
        ),
        smem=(0, 9),
        nbytes=2 * MIB,
        scratch=[pltpu.VMEM((block, w_final.shape[1]), F32)],
    )
    routed = lax.all_to_all(slot_rows, "mdl", split_axis=0, concat_axis=0, tiled=True)
    upsampled = call(
        up_body, shape((16 * CAP, w_up.shape[1]), BF), (routed, w_up), nbytes=MIB
    )
    return (hidden_out, next_state, upsampled)


def solution(mesh):
    return jax.shard_map(
        shards,
        mesh=mesh,
        in_specs=(
            P("ctx", "mdl"),
            P(),
            P(),
            P(),
            P(None, "mdl"),
            P(None, "mdl"),
            P(None, "mdl"),
            P("mdl", None),
            P("ctx", "mdl"),
            P("ctx", "mdl"),
            P(),
            P(),
            P(("ctx", "mdl"), None),
            P(("ctx", "mdl"), None),
            P(("ctx", "mdl"), None),
            P(),
        ),
        out_specs=(P(("ctx", "mdl"), None), P(("ctx", "mdl"), None), P(("ctx", "mdl"), None)),
        check_vma=False,
    )
```
